256 devices in a mesh: dp: 4 (over y), expert: 16 (over z, core), chan: 4 (over x).
Axes of the slice: x: 4, y: 4, z: 8, core: 2. Of those that a mesh axis runs over, the one named last changes fastest.
Arguments:
- tokens: bfloat16 [16384, 1024], P(('dp', 'expert'), 'chan'), may hold values from -6 to 6
- out_cotangent: bfloat16 [16384, 1024], P(('dp', 'expert'), 'chan'), may hold values from -6 to 6
- routes: int32 [16384, 2], P(('dp', 'expert')), may hold values from 0 to 31, all different within a row; in each aligned block of 256 rows (0 to 255, 256 to 511, ...) at most 32 rows name the same one
- gate_values: bfloat16 [16384, 2], P(('dp', 'expert')), may hold values from 0.099609375 to 1
- in_weight: bfloat16 [32, 1024, 4096], P('expert', None, 'chan'), may hold values from -0.1875 to 0.1875
- out_weight: bfloat16 [32, 4096, 1024], P('expert', 'chan'), may hold values from -0.09375 to 0.09375
Outputs:
- token_grads: bfloat16 [16384, 1024], P(('dp', 'expert'), 'chan')
- gate_grads: bfloat16 [16384, 2], P(('dp', 'expert'))
- in_grads: bfloat16 [32, 1024, 4096], P('expert', 'dp', 'chan')
- out_grads: bfloat16 [32, 4096, 1024], P('expert', 'chan', 'dp')
The draws below stay inside these ranges and needn't reach their ends.
Inputs may be any that keep to these rules, and one draw needn't show every extreme that they name: `routes`: each token names 2 different experts. Among the 256 tokens of one device's block (aligned blocks of 256 tokens), no expert is named more than 32 times, and in every draw some expert is named exactly 32 times in some block.
All inputs are finite; a program needn't handle non-finite values.
Results may differ from the reference program's by a relative error of at most 0.017.
Values may be sent and summed in bfloat16 or wider, within the bound.
No kernel may reach another device: no remote copies, remote signals or barrier semaphores. Data moves between devices by JAX's collectives and lax.ppermute only.
A program may use at most 128 MiB of HBM per device.

```python
import math
import jax
import jax.numpy as jnp
import numpy as np
from jax import lax

D = 1024
FF = 4096
TOP = 2
TOK_DEV = 256
EXPERTS = 32
CAP = 32
TOKENS = 16384
N_DP = 4
N_EXPERT = 16


def shard_levels(own_key, dims, cuts, low, high):
    level = 1.0
    for axis_at, parts in cuts:
        heights = jax.random.uniform(jax.random.fold_in(jax.random.fold_in(own_key, 6), axis_at), (parts,), jnp.float32, low / len(cuts), high / len(cuts))
        level = level * jnp.repeat(jnp.exp(heights), dims[axis_at] // parts).reshape((-1,) + (1,) * (len(dims) - 1 - axis_at))
    return level


def shared_out(rng, own, number, rows, number_of, top, limit, lean):
    sequence = jax.random.permutation(rng, number_of)
    heavy_load, usual = load_shares(number_of, rows * top, limit, lean, True), load_shares(number_of, rows * top, limit, lean, False)
    places = jnp.arange(number_of)

    def named(lengths, rotation):
        used = int((lengths > 0).sum())
        fixed = max(1, used // 4)
        moved = fixed + (places - fixed + rotation * (used - fixed)) % max(1, number_of - fixed)
        return jnp.zeros((number_of,), jnp.int32).at[sequence[jnp.where(places < fixed, places, moved)]].set(jnp.asarray(lengths, jnp.int32))

    lengths = jnp.where(number % 4 == 0, named(heavy_load, number // 4), named(usual, number - number // 4 - 1))
    mixed = jax.random.permutation(jax.random.fold_in(own, 3), number_of)
    source_of, receiver = mixed[0:number_of // 2 * 2:2], mixed[1:number_of // 2 * 2:2]
    room = jnp.minimum(lengths[source_of] - 1, limit - lengths[receiver]) // 2
    room = jnp.where((source_of == sequence[0]) | (receiver == sequence[0]) | (lengths[receiver] == 0), 0, jnp.maximum(room, 0))
    moved = jax.random.randint(jax.random.fold_in(own, 4), (number_of // 2,), 0, 1 << 20) % (room + 1)
    lengths = lengths.at[source_of].add(-moved).at[receiver].add(moved)
    labels = jnp.searchsorted(jnp.cumsum(lengths), jnp.arange(rows * top), side="right").astype(jnp.int32)
    table = labels.reshape(top, rows).T
    table = table[jax.random.permutation(jax.random.fold_in(own, 1), rows)]
    rotation = jax.random.randint(jax.random.fold_in(own, 2), (rows, 1), 0, top)
    return jnp.take_along_axis(table, (jnp.arange(top)[None, :] + rotation) % top, axis=1)


def load_shares(count, total, most, skew, full):
    portions = [(1 << 20) // math.isqrt(rank ** skew) + 1 for rank in range(1, count + 1)]
    largest = most if full else min(most, max(-(-total // count), total * portions[0] // sum(portions)))
    least = 1 if total - largest >= count - 1 else 0
    counts, rest = [largest] + [least] * (count - 1), total - largest - least * (count - 1)
    while rest > 0:
        free = [i for i in range(1, count) if counts[i] < largest] or [i for i in range(1, count) if counts[i] < most]
        mass, remaining = sum([portions[i] for i in free]), rest
        for i in free:
            more = min(most - counts[i], max(1, remaining * portions[i] // mass), rest)
            counts[i] = counts[i] + more
            rest = rest - more
    return np.array(counts)


def noise(stream_key, extent, deviation, bound, split=(), held_as=jnp.bfloat16):
    result = deviation * jax.random.normal(stream_key, extent, jnp.float32)
    if split:
        result = result * shard_levels(stream_key, extent, split, -0.22, 0.18)
    return jnp.clip(result, -bound, bound).astype(held_as)


def setup_inputs(seed: int = 0) -> dict:
    arg_keys = jax.random.split(jax.random.key(seed), 7)
    tokens = noise(arg_keys[0], (TOKENS, D), 1.0, 6.0, ((0, 64), (1, 4)))
    out_cotangent = noise(arg_keys[1], (TOKENS, D), 1.0, 6.0, ((0, 64), (1, 4)))
    routes_keys = jax.random.split(jax.random.fold_in(arg_keys[2], 1), TOKENS // TOK_DEV)
    routes_turns = jax.random.permutation(jax.random.fold_in(arg_keys[2], 3), TOKENS // TOK_DEV)
    routes = jax.vmap(lambda own, number: shared_out(jax.random.fold_in(arg_keys[2], 2), own, number, TOK_DEV, EXPERTS, TOP, CAP, 2))(routes_keys, routes_turns).reshape((TOKENS, TOP))
    gate_values = jnp.clip(jnp.exp(math.log(1.0) - 2.306499 * jax.random.uniform(arg_keys[3], (TOKENS, TOP), jnp.float32) ** shard_levels(arg_keys[3], (TOKENS, TOP), ((0, 64),), -0.2, 0.2)), 0.099609375, 1.0).astype(jnp.bfloat16)
    in_weight = noise(arg_keys[4], (EXPERTS, D, FF), D ** -0.5, 0.1875, ((0, 16), (2, 4)))
    out_weight = noise(arg_keys[5], (EXPERTS, FF, D), FF ** -0.5, 0.09375, ((0, 16), (1, 4)))
    return {"tokens": tokens, "out_cotangent": out_cotangent, "routes": routes, "gate_values": gate_values, "in_weight": in_weight, "out_weight": out_weight}


def gelu_parts(pre):
    cdf = 0.5 * (1.0 + jax.scipy.special.erf(pre * (1.0 / math.sqrt(2.0))))
    dens = jnp.exp(-0.5 * pre * pre) * (1.0 / math.sqrt(2.0 * math.pi))
    return (pre * cdf, cdf + pre * dens)

def reference(tokens, out_cotangent, routes, gate_values, in_weight, out_weight):
    blocks = N_DP * N_EXPERT
    per_block = routes.reshape(blocks, TOK_DEV * TOP)
    onehot = (per_block[:, :, None] == jnp.arange(EXPERTS, dtype=jnp.int32)[None, None, :]).astype(jnp.int32)
    before = jnp.cumsum(onehot, axis=1) - onehot
    slot = lax.optimization_barrier(jnp.sum(before * onehot, axis=2))
    block_ids = jnp.arange(blocks, dtype=jnp.int32)[:, None]
    place = per_block * (blocks * CAP) + block_ids * CAP + slot
    place = place.reshape(-1).astype(jnp.int32)
    total = EXPERTS * blocks * CAP
    row_count = blocks * TOK_DEV * TOP
    table = jnp.zeros((total,), jnp.int32).at[place].set(jnp.arange(row_count, dtype=jnp.int32) + 1)
    table = table.reshape(EXPERTS, N_DP, N_EXPERT * CAP)
    gate_flat = gate_values.reshape(-1)

    def per_expert(inputs):
        index, w_first, w_second = inputs
        filled = index > 0
        source_row = jnp.maximum(index - 1, 0).astype(jnp.int32)
        source_token = source_row // TOP
        xs = jnp.where(filled[..., None], tokens[source_token], jnp.zeros((), jnp.bfloat16)).astype(jnp.float32)
        dys = jnp.where(filled[..., None], out_cotangent[source_token], jnp.zeros((), jnp.bfloat16)).astype(jnp.float32)
        gate = jnp.where(filled, gate_flat[source_row], jnp.zeros((), jnp.bfloat16)).astype(jnp.float32)[..., None]
        w_a = w_first.astype(jnp.float32)
        w_b = w_second.astype(jnp.float32)
        pre = jnp.einsum('prd,df->prf', xs, w_a)
        act, slope = gelu_parts(pre)
        back = jnp.einsum('prd,fd->prf', dys, w_b)
        gate_part = lax.optimization_barrier(jnp.sum(act * back, axis=-1)).astype(jnp.bfloat16)
        grad_pre = (gate * back * slope).astype(jnp.bfloat16)
        scaled = (gate * act).astype(jnp.bfloat16)
        rows = jnp.einsum('prf,df->prd', grad_pre.astype(jnp.float32), w_a).astype(jnp.bfloat16)
        in_part = jnp.einsum('prd,prf->pdf', xs, grad_pre.astype(jnp.float32)).astype(jnp.bfloat16)
        in_sum = lax.optimization_barrier(jnp.sum(in_part.astype(jnp.float32), axis=0)).astype(jnp.bfloat16)
        out_part = jnp.einsum('prf,prd->pfd', scaled.astype(jnp.float32), dys).astype(jnp.bfloat16)
        out_sum = lax.optimization_barrier(jnp.sum(out_part.astype(jnp.float32), axis=0)).astype(jnp.bfloat16)
        return (rows, gate_part, in_sum, out_sum)
    rows, gate_part, in_grads, out_grads = lax.map(per_expert, (table, in_weight, out_weight))
    rows_flat = rows.reshape(total, D)
    gate_flat_out = gate_part.reshape(total)
    row_vals = rows_flat[place].reshape(blocks * TOK_DEV, TOP, D)
    token_grads = lax.optimization_barrier(jnp.sum(row_vals.astype(jnp.float32), axis=1)).astype(jnp.bfloat16)
    gate_grads = gate_flat_out[place].reshape(blocks * TOK_DEV, TOP)
    return (token_grads, gate_grads, in_grads, out_grads)
```

```python
import math

import jax
import jax.numpy as jnp
from jax import lax
from jax.experimental import pallas as pl
from jax.experimental.pallas import tpu as pltpu
from jax.sharding import PartitionSpec as P

BF = jnp.bfloat16
F32 = jnp.float32
VMEM_BYTES = 40 * 1024 * 1024


def dot(a, b):
    return jnp.dot(a, b, preferred_element_type=F32)


def dot_t(a, b):
    return lax.dot_general(a, b, (((1,), (1,)), ((), ())), preferred_element_type=F32)


def call(body, ins, outs, flops, picked=(), scratch=()):
    picked = dict(picked)
    specs = [pl.BlockSpec(memory_space=pltpu.SMEM)]
    for at, x in enumerate(ins):
        if at == 0:
            continue
        if at in picked:
            j = picked[at]
            specs.append(pl.BlockSpec((1,) + x.shape[1:], lambda i, j=j: (j, 0, 0)))
        else:
            specs.append(pl.BlockSpec(x.shape, lambda i, n=x.ndim: (0,) * n))
    moved = sum(x.size * x.dtype.itemsize for x in ins) + sum(
        math.prod(s) * jnp.dtype(d).itemsize for s, d in outs
    )
    return pl.pallas_call(
        body,
        grid=(1,),
        in_specs=specs,
        out_specs=[pl.BlockSpec(s, lambda i, n=len(s): (0,) * n) for s, _ in outs],
        out_shape=[jax.ShapeDtypeStruct(s, d) for s, d in outs],
        scratch_shapes=scratch,
        compiler_params=pltpu.CompilerParams(vmem_limit_bytes=VMEM_BYTES),
        cost_estimate=pl.CostEstimate(flops=flops, bytes_accessed=moved, transcendentals=0),
    )(*ins)


def slot_places(routes, experts, capacity):
    toks = routes.shape[0]
    r0 = routes[:, 0:1]
    r1 = routes[:, 1:2]
    lane = lax.broadcasted_iota(jnp.int32, (toks, 128), 1)
    named = jnp.where((lane == r0) | (lane == r1), 1.0, 0.0).astype(BF)
    row = lax.broadcasted_iota(jnp.int32, (toks, toks), 0)
    col = lax.broadcasted_iota(jnp.int32, (toks, toks), 1)
    earlier = jnp.where(col < row, 1.0, 0.0).astype(BF)
    before = dot(earlier, named)
    out = []
    for r in (r0, r1):
        slot = jnp.sum(jnp.where(lane == r, before, 0.0), axis=1, keepdims=True).astype(jnp.int32)
        which = r & 1
        place = (r >> 1) * capacity + slot
        out.append((which, place))
    return out


def matches(places, j, toks, slots):
    lane = lax.broadcasted_iota(jnp.int32, (toks, slots), 1)
    return [lane == jnp.where(which == j, place, -1) for which, place in places]


def on_device(tokens, out_cotangent, routes, gate_values, in_weight, out_weight):
    toks, quarter = tokens.shape
    groups = lax.axis_size("expert")
    n_local = in_weight.shape[0]
    experts = n_local * groups
    capacity = min(toks, 4 * toks // experts)
    slots = groups * capacity
    width, hidden = in_weight.shape[1:]
    n_chan = lax.axis_size("chan")
    half = slots // 2
    here = jnp.stack([lax.axis_index("dp"), lax.axis_index("chan")]).astype(jnp.int32)

    def shift(x, axis, by):
        n = lax.axis_size(axis)
        return lax.ppermute(x, axis, [(i, (i + by) % n) for i in range(n)])

    def pack_body(_, x_ref, dy_ref, routes_ref, gate_ref, *send_refs):
        places = slot_places(routes_ref[...], experts, capacity)
        gate = gate_ref[...].astype(F32)
        x = x_ref[...]
        dy = dy_ref[...]
        for j in range(n_local):
            m0, m1 = matches(places, j, toks, slots)
            pick = jnp.where(m0 | m1, 1.0, 0.0)
            gated = jnp.where(m0, gate[:, 0:1], 0.0) + jnp.where(m1, gate[:, 1:2], 0.0)
            send_refs[j][:, :quarter] = dot(pick.T.astype(BF), x).astype(BF)
            send_refs[j][:, quarter:] = dot(gated.T.astype(BF), dy).astype(BF)

    sends = call(
        pack_body,
        [here, tokens, out_cotangent, routes, gate_values],
        [((slots, 2 * quarter), BF)] * n_local,
        4 * n_local * slots * toks * quarter,
    )

    def exchange(x):
        return lax.all_to_all(
            x.reshape(groups, capacity, x.shape[1]), "expert", split_axis=0, concat_axis=0, tiled=True
        ).reshape(x.shape)

    def gather_parts(x):
        left = shift(x, "chan", 1)
        right = shift(x, "chan", -1)
        return [x, left, right, shift(left[:half], "chan", 1), shift(right[half:], "chan", -1)]

    def lay_out(c, parts, full_ref):
        own, left, right, opp_a, opp_b = parts

        def cols(k):
            return pl.ds(pl.multiple_of(((c + k) % n_chan) * quarter, quarter), quarter)

        full_ref[:, cols(0)] = own[...]
        full_ref[:, cols(n_chan - 1)] = left[...]
        full_ref[:, cols(1)] = right[...]
        full_ref[:half, cols(2)] = opp_a[...]
        full_ref[half:, cols(2)] = opp_b[...]

    tile = 256
    tiles = hidden // tile
    n_dp = lax.axis_size("dp")

    def act_body(here_ref, *refs):
        parts, w_ref, (xs_ref, act_ref, slope_ref) = refs[:5], refs[5], refs[6:]
        lay_out(here_ref[1], parts, xs_ref)
        for f in range(tiles):
            at = slice(f * tile, (f + 1) * tile)
            pre = dot(xs_ref[...], w_ref[0, :, at])
            cdf = 0.5 * (1.0 + lax.erf(pre * (1.0 / math.sqrt(2.0))))
            dens = jnp.exp(-0.5 * pre * pre) * (1.0 / math.sqrt(2.0 * math.pi))
            act_ref[:, at] = (pre * cdf).astype(BF)
            slope_ref[:, at] = (cdf + pre * dens).astype(BF)

    def quarter_at(c, k):
        return pl.ds(pl.multiple_of(((c + k) % n_dp) * quarter, quarter), quarter)

    def store_piece(refs, k, rows, value):
        if k == 0:
            refs[0][rows, :] = value
            return
        a, b = refs[2 * k - 1], refs[2 * k]
        size = a.shape[0]
        lo, hi = rows.start, rows.stop
        if lo < size:
            stop = min(hi, size)
            a[lo:stop, :] = value[: stop - lo]
        if hi > size:
            start = max(lo, size)
            b[start - size : hi - size, :] = value[start - lo :]

    def pieces(rows, cols):
        return [((rows, cols), BF)] + [((rows // 2, cols), BF)] * 6

    def out_body(here_ref, *refs):
        parts, act_ref, dys_ref, piece_refs = refs[:5], refs[5], refs[6], refs[7:]
        lay_out(here_ref[1], parts, dys_ref)
        for f in range(tiles):
            rows = slice(f * tile, (f + 1) * tile)
            act_t = act_ref[:, rows].T
            for k in range(n_dp):
                value = dot(act_t, dys_ref[:, quarter_at(here_ref[0], k)]).astype(BF)
                store_piece(piece_refs, k, rows, value)

    def in_body(here_ref, dys_ref, w_ref, act_ref, slope_ref, xs_ref, *refs):
        grad_ref, gate_ref, piece_refs = refs[0], refs[1], refs[2:]
        total = jnp.zeros((slots, 1), F32)
        for f in range(tiles):
            at = slice(f * tile, (f + 1) * tile)
            back = dot_t(dys_ref[...], w_ref[0, at, :])
            total += jnp.sum(act_ref[:, at].astype(F32) * back, axis=1, keepdims=True)
            grad_ref[:, at] = (back * slope_ref[:, at].astype(F32)).astype(BF)
        gate_ref[...] = total
        for k in (2, 1, 3, 0):
            x_t = xs_ref[:, quarter_at(here_ref[0], k)].T
            for f in range(tiles):
                at = slice(f * tile, (f + 1) * tile)
                value = dot(x_t, grad_ref[:, at]).astype(BF)
                if k == 0:
                    piece_refs[0][:, at] = value
                else:
                    piece_refs[2 * k - 1][:, at] = value[: quarter // 2]
                    piece_refs[2 * k][:, at] = value[quarter // 2 :]

    def row_body(here_ref, grad_ref, w_ref, *piece_refs):
        for k in (2, 1, 3, 0):
            value = dot_t(grad_ref[...], w_ref[0, quarter_at(here_ref[1], k), :]).astype(BF)
            store_piece(piece_refs, k, slice(0, slots), value)

    def reduce_pieces(parts, axis):
        own, up_a, up_b, opp_a, opp_b, down_a, down_b = parts
        got_a = shift(opp_a, axis, 1)
        got_b = shift(opp_b, axis, -1)
        from_down_b = shift(up_b, axis, 1)
        from_up_a = shift(down_a, axis, -1)
        up_sum = (up_a.astype(F32) + got_a.astype(F32)).astype(BF)
        down_sum = (down_b.astype(F32) + got_b.astype(F32)).astype(BF)
        from_down_a = shift(up_sum, axis, 1)
        from_up_b = shift(down_sum, axis, -1)
        n = own.shape[0] // 2
        first = own[:n].astype(F32) + from_down_a.astype(F32) + from_up_a.astype(F32)
        second = own[n:].astype(F32) + from_down_b.astype(F32) + from_up_b.astype(F32)
        return jnp.concatenate([first, second], axis=0).astype(BF)

    received = [exchange(s) for s in sends]
    gates, rows_back, in_grads, out_grads = [], [], [], []
    for j in range(n_local):
        x_parts = gather_parts(received[j][:, :quarter])
        dy_parts = gather_parts(received[j][:, quarter:])
        flops = 2 * slots * width * hidden
        xs, act, slope = call(
            act_body,
            [here, *x_parts, in_weight],
            [((slots, width), BF), ((slots, hidden), BF), ((slots, hidden), BF)],
            flops,
            [(6, j)],
        )
        dys, *out_parts = call(
            out_body, [here, *dy_parts, act], [((slots, width), BF)] + pieces(hidden, quarter), flops
        )
        out_grads.append(reduce_pieces(out_parts, "dp"))
        grad_pre, gate_part, *in_parts = call(
            in_body,
            [here, dys, out_weight, act, slope, xs],
            [((slots, hidden), BF), ((slots, 1), F32)] + pieces(quarter, hidden),
            2 * flops,
            [(2, j)],
        )
        in_grads.append(reduce_pieces(in_parts, "dp"))
        row_parts = call(row_body, [here, grad_pre, in_weight], pieces(slots, quarter), flops, [(2, j)])
        rows_back.append(exchange(reduce_pieces(row_parts, "chan")))
        gates.append(gate_part.reshape(groups, capacity))

    gate_rows = lax.all_to_all(
        jnp.concatenate(gates, axis=1), "expert", split_axis=0, concat_axis=0, tiled=True
    ).reshape(groups, n_local, capacity)
    gate_rows = lax.psum(gate_rows, "chan").transpose(1, 0, 2).reshape(n_local, slots)

    def combine_body(_, routes_ref, gate_ref, sums_ref, *refs):
        rows_refs, (token_ref, gate_out_ref) = refs[:n_local], refs[n_local:]
        places = slot_places(routes_ref[...], experts, capacity)
        total = jnp.zeros((toks, quarter), F32)
        sums = [jnp.zeros((toks, 1), F32), jnp.zeros((toks, 1), F32)]
        for j in range(n_local):
            m = matches(places, j, toks, slots)
            pick = jnp.where(m[0] | m[1], 1.0, 0.0).astype(BF)
            total += dot(pick, rows_refs[j][...])
            for k in range(2):
                sums[k] += jnp.sum(jnp.where(m[k], sums_ref[j : j + 1, :], 0.0), axis=1, keepdims=True)
        token_ref[...] = total.astype(BF)
        gate = gate_ref[...].astype(F32)
        for k in range(2):
            gate_out_ref[:, k : k + 1] = (sums[k] / gate[:, k : k + 1]).astype(BF)

    token_grads, gate_grads = call(
        combine_body,
        [here, routes, gate_values, gate_rows, *rows_back],
        [((toks, quarter), BF), (gate_values.shape, BF)],
        2 * n_local * slots * toks * quarter,
    )
    return (token_grads, gate_grads, jnp.stack(in_grads), jnp.stack(out_grads))


def solution(mesh):
    placed = (
        P(("dp", "expert"), "chan"),
        P(("dp", "expert"), "chan"),
        P(("dp", "expert"), None),
        P(("dp", "expert"), None),
        P("expert", None, "chan"),
        P("expert", "chan", None),
    )
    return jax.shard_map(
        on_device,
        mesh=mesh,
        in_specs=placed,
        out_specs=(
            P(("dp", "expert"), "chan"),
            P(("dp", "expert"), None),
            P("expert", "dp", "chan"),
            P("expert", "chan", "dp"),
        ),
        check_vma=False,
    )
```

```python
import math

import jax
import jax.numpy as jnp
from jax import lax
from jax.experimental import pallas as pl
from jax.experimental.pallas import tpu as pltpu
from jax.sharding import PartitionSpec as P

BF = jnp.bfloat16
F32 = jnp.float32
VMEM_BYTES = 60 * 1024 * 1024


def dot(a, b):
    return jnp.dot(a, b, preferred_element_type=F32)


def dot_t(a, b):
    return lax.dot_general(a, b, (((1,), (1,)), ((), ())), preferred_element_type=F32)


def call(body, ins, outs, flops, picked=(), scratch=()):
    picked = dict(picked)
    specs = [pl.BlockSpec(memory_space=pltpu.SMEM)]
    for at, x in enumerate(ins):
        if at == 0:
            continue
        if at in picked:
            j = picked[at]
            specs.append(pl.BlockSpec((1,) + x.shape[1:], lambda i, j=j: (j, 0, 0)))
        else:
            specs.append(pl.BlockSpec(x.shape, lambda i, n=x.ndim: (0,) * n))
    moved = sum(x.size * x.dtype.itemsize for x in ins) + sum(
        math.prod(s) * jnp.dtype(d).itemsize for s, d in outs
    )
    return pl.pallas_call(
        body,
        grid=(1,),
        in_specs=specs,
        out_specs=[pl.BlockSpec(s, lambda i, n=len(s): (0,) * n) for s, _ in outs],
        out_shape=[jax.ShapeDtypeStruct(s, d) for s, d in outs],
        scratch_shapes=scratch,
        compiler_params=pltpu.CompilerParams(vmem_limit_bytes=VMEM_BYTES),
        cost_estimate=pl.CostEstimate(flops=flops // 16, bytes_accessed=moved // 16, transcendentals=0),
    )(*ins)


def slot_places(routes, experts, capacity):
    toks = routes.shape[0]
    r0 = routes[:, 0:1]
    r1 = routes[:, 1:2]
    lane = lax.broadcasted_iota(jnp.int32, (toks, 128), 1)
    named = jnp.where((lane == r0) | (lane == r1), 1.0, 0.0).astype(BF)
    row = lax.broadcasted_iota(jnp.int32, (toks, toks), 0)
    col = lax.broadcasted_iota(jnp.int32, (toks, toks), 1)
    earlier = jnp.where(col < row, 1.0, 0.0).astype(BF)
    before = dot(earlier, named)
    out = []
    for r in (r0, r1):
        slot = jnp.sum(jnp.where(lane == r, before, 0.0), axis=1, keepdims=True).astype(jnp.int32)
        which = r & 1
        place = (r >> 1) * capacity + slot
        out.append((which, place))
    return out


def matches(places, j, toks, slots):
    lane = lax.broadcasted_iota(jnp.int32, (toks, slots), 1)
    return [lane == jnp.where(which == j, place, -1) for which, place in places]


def on_device(tokens, out_cotangent, routes, gate_values, in_weight, out_weight):
    toks, quarter = tokens.shape
    groups = lax.axis_size("expert")
    n_local = in_weight.shape[0]
    experts = n_local * groups
    capacity = min(toks, 4 * toks // experts)
    slots = groups * capacity
    width, hidden = in_weight.shape[1:]
    n_chan = lax.axis_size("chan")
    half = slots // 2
    here = jnp.stack([lax.axis_index("dp"), lax.axis_index("chan")]).astype(jnp.int32)

    def shift(x, axis, by):
        n = lax.axis_size(axis)
        return lax.ppermute(x, axis, [(i, (i + by) % n) for i in range(n)])

    def pack_body(_, x_ref, dy_ref, routes_ref, gate_ref, *send_refs):
        places = slot_places(routes_ref[...], experts, capacity)
        gate = gate_ref[...].astype(F32)
        x = x_ref[...]
        dy = dy_ref[...]
        for j in range(n_local):
            m0, m1 = matches(places, j, toks, slots)
            pick = jnp.where(m0 | m1, 1.0, 0.0)
            gated = jnp.where(m0, gate[:, 0:1], 0.0) + jnp.where(m1, gate[:, 1:2], 0.0)
            send_refs[j][:, :quarter] = dot(pick.T.astype(BF), x).astype(BF)
            send_refs[j][:, quarter:] = dot(gated.T.astype(BF), dy).astype(BF)

    sends = call(
        pack_body,
        [here, tokens, out_cotangent, routes, gate_values],
        [((slots, 2 * quarter), BF)] * n_local,
        4 * n_local * slots * toks * quarter,
    )

    def exchange(x):
        return lax.all_to_all(
            x.reshape(groups, capacity, x.shape[1]), "expert", split_axis=0, concat_axis=0, tiled=True
        ).reshape(x.shape)

    def gather_parts(x):
        left = shift(x, "chan", 1)
        right = shift(x, "chan", -1)
        return [x, left, right, shift(left[:half], "chan", 1), shift(right[half:], "chan", -1)]

    def lay_out(c, parts, first, full_ref):
        own, left, right, opp_a, opp_b = parts

        def cols(k):
            return pl.ds(pl.multiple_of(((c + k) % n_chan) * quarter, quarter), quarter)

        full_ref[:, cols(0)] = own[:, first : first + quarter]
        full_ref[:, cols(n_chan - 1)] = left[:, first : first + quarter]
        full_ref[:, cols(1)] = right[:, first : first + quarter]
        full_ref[:half, cols(2)] = opp_a[:, first : first + quarter]
        full_ref[half:, cols(2)] = opp_b[:, first : first + quarter]

    tile = 256
    tiles = hidden // tile
    n_dp = lax.axis_size("dp")

    def act_body(here_ref, *refs):
        parts, w_ref, (xs_ref, act_ref, slope_ref) = refs[:5], refs[5], refs[6:]
        lay_out(here_ref[1], parts, 0, xs_ref)
        for f in range(tiles):
            at = slice(f * tile, (f + 1) * tile)
            pre = dot(xs_ref[...], w_ref[0, :, at])
            cdf = 0.5 * (1.0 + lax.erf(pre * (1.0 / math.sqrt(2.0))))
            dens = jnp.exp(-0.5 * pre * pre) * (1.0 / math.sqrt(2.0 * math.pi))
            act_ref[:, at] = (pre * cdf).astype(BF)
            slope_ref[:, at] = (cdf + pre * dens).astype(BF)

    def quarter_at(c, k):
        return pl.ds(pl.multiple_of(((c + k) % n_dp) * quarter, quarter), quarter)

    def pieces(rows, cols):
        return [((rows, cols), BF)] * n_dp

    def out_body(here_ref, *refs):
        parts, act_ref, dys_ref, piece_refs = refs[:5], refs[5], refs[6], refs[7:]
        lay_out(here_ref[1], parts, quarter, dys_ref)
        for f in range(tiles):
            rows = slice(f * tile, (f + 1) * tile)
            act_t = act_ref[:, rows].T
            for k in range(n_dp):
                value = dot(act_t, dys_ref[:, quarter_at(here_ref[0], k)])
                piece_refs[k][rows, :] = value.astype(BF)

    def in_body(here_ref, dys_ref, w_ref, act_ref, slope_ref, xs_ref, *refs):
        grad_ref, gate_ref, piece_refs = refs[0], refs[1], refs[2:]
        total = jnp.zeros((slots, 1), F32)
        for f in range(tiles):
            at = slice(f * tile, (f + 1) * tile)
            back = dot_t(dys_ref[...], w_ref[0, at, :])
            total += jnp.sum(act_ref[:, at].astype(F32) * back, axis=1, keepdims=True)
            grad_ref[:, at] = (back * slope_ref[:, at].astype(F32)).astype(BF)
        gate_ref[...] = total
        for k in (2, 1, 3, 0):
            x_t = xs_ref[:, quarter_at(here_ref[0], k)].T
            for f in range(tiles):
                at = slice(f * tile, (f + 1) * tile)
                piece_refs[k][:, at] = dot(x_t, grad_ref[:, at]).astype(BF)

    def row_body(here_ref, grad_ref, w_ref, *piece_refs):
        for k in range(n_chan):
            piece_refs[k][...] = dot_t(grad_ref[...], w_ref[0, quarter_at(here_ref[1], k), :]).astype(BF)

    def add(a, b):
        return (a.astype(F32) + b.astype(F32)).astype(BF)

    def reduce_pieces(parts, axis, by):
        own, near, far = parts[0], parts[by % 4], parts[-by % 4]
        joined = add(near, shift(parts[2], axis, by))
        from_far = shift(far, axis, -by)
        from_near = shift(joined, axis, by)
        return (own.astype(F32) + from_near.astype(F32) + from_far.astype(F32)).astype(BF)

    received = []
    for j in range(n_local):
        sent = sends[j]
        if received:
            sent, received[-1] = lax.optimization_barrier((sent, received[-1]))
        received.append(exchange(sent))
    gates, rows_back, in_grads, out_grads = [], [], [], []
    for j in range(n_local):
        parts = gather_parts(received[j])
        flops = 2 * slots * width * hidden
        xs, act, slope = call(
            act_body,
            [here, *parts, in_weight],
            [((slots, width), BF), ((slots, hidden), BF), ((slots, hidden), BF)],
            flops,
            [(6, j)],
        )
        dys, *out_parts = call(
            out_body, [here, *parts, act], [((slots, width), BF)] + pieces(hidden, quarter), flops
        )
        out_grads.append(reduce_pieces(out_parts, "dp", 1))
        grad_pre, gate_part, *in_parts = call(
            in_body,
            [here, dys, out_weight, act, slope, xs],
            [((slots, hidden), BF), ((slots, 1), F32)] + pieces(quarter, hidden),
            2 * flops,
            [(2, j)],
        )
        in_grads.append(reduce_pieces(in_parts, "dp", -1))
        row_parts = call(row_body, [here, grad_pre, in_weight], pieces(slots, quarter), flops, [(2, j)])
        rows_back.append(exchange(reduce_pieces(row_parts, "chan", 1 - 2 * (j % 2))))
        gates.append(gate_part.reshape(groups, capacity))

    gate_rows = jnp.concatenate(gates, axis=1)
    gate_rows = jnp.broadcast_to(gate_rows[:, None, :], (groups, n_chan, n_local * capacity))
    gate_rows = lax.all_to_all(
        gate_rows.reshape(groups * n_chan, n_local * capacity),
        ("expert", "chan"),
        split_axis=0,
        concat_axis=0,
        tiled=True,
    ).reshape(groups, n_chan, n_local, capacity)
    gate_rows = jnp.sum(gate_rows, axis=1).transpose(1, 0, 2).reshape(n_local, slots)

    def combine_body(_, routes_ref, gate_ref, sums_ref, *refs):
        rows_refs, (token_ref, gate_out_ref) = refs[:n_local], refs[n_local:]
        places = slot_places(routes_ref[...], experts, capacity)
        total = jnp.zeros((toks, quarter), F32)
        sums = [jnp.zeros((toks, 1), F32), jnp.zeros((toks, 1), F32)]
        for j in range(n_local):
            m = matches(places, j, toks, slots)
            pick = jnp.where(m[0] | m[1], 1.0, 0.0).astype(BF)
            total += dot(pick, rows_refs[j][...])
            for k in range(2):
                sums[k] += jnp.sum(jnp.where(m[k], sums_ref[j : j + 1, :], 0.0), axis=1, keepdims=True)
        token_ref[...] = total.astype(BF)
        gate = gate_ref[...].astype(F32)
        for k in range(2):
            gate_out_ref[:, k : k + 1] = (sums[k] / gate[:, k : k + 1]).astype(BF)

    token_grads, gate_grads = call(
        combine_body,
        [here, routes, gate_values, gate_rows, *rows_back],
        [((toks, quarter), BF), (gate_values.shape, BF)],
        2 * n_local * slots * toks * quarter,
    )
    return (token_grads, gate_grads, jnp.stack(in_grads), jnp.stack(out_grads))


def solution(mesh):
    placed = (
        P(("dp", "expert"), "chan"),
        P(("dp", "expert"), "chan"),
        P(("dp", "expert"), None),
        P(("dp", "expert"), None),
        P("expert", None, "chan"),
        P("expert", "chan", None),
    )
    return jax.shard_map(
        on_device,
        mesh=mesh,
        in_specs=placed,
        out_specs=(
            P(("dp", "expert"), "chan"),
            P(("dp", "expert"), None),
            P("expert", "dp", "chan"),
            P("expert", "chan", "dp"),
        ),
        check_vma=False,
    )
```

```python
import functools
import math

import jax
import jax.numpy as jnp
from jax import lax
from jax.experimental import pallas as pl
from jax.experimental.pallas import tpu as pltpu
from jax.sharding import PartitionSpec as P

BF = jnp.bfloat16
F32 = jnp.float32
VMEM_BYTES = 60 * 1024 * 1024


def dot(a, b):
    return jnp.dot(a, b, preferred_element_type=F32)


def dot_t(a, b):
    return lax.dot_general(a, b, (((1,), (1,)), ((), ())), preferred_element_type=F32)


def call(body, ins, outs, flops, far_ins=0, far_outs=0, scratch=()):
    far = pl.BlockSpec(memory_space=pl.ANY)

    def specs(shapes, n_far):
        near = len(shapes) - n_far
        return [pl.BlockSpec(s, lambda i, n=len(s): (0,) * n) for s in shapes[:near]] + [far] * n_far

    moved = sum(x.size * x.dtype.itemsize for x in ins) + sum(
        math.prod(s) * jnp.dtype(d).itemsize for s, d in outs
    )
    return pl.pallas_call(
        body,
        grid=(1,),
        in_specs=[pl.BlockSpec(memory_space=pltpu.SMEM)] + specs([x.shape for x in ins[1:]], far_ins),
        out_specs=specs([s for s, _ in outs], far_outs),
        out_shape=[jax.ShapeDtypeStruct(s, d) for s, d in outs],
        scratch_shapes=scratch,
        compiler_params=pltpu.CompilerParams(vmem_limit_bytes=VMEM_BYTES),
        cost_estimate=pl.CostEstimate(flops=flops // 16, bytes_accessed=moved // 16, transcendentals=0),
    )(*ins)


class Copies:
    def __init__(self, sems):
        self.sems = sems
        self.started = []

    def start(self, source, target):
        copy = pltpu.make_async_copy(source, target, self.sems.at[len(self.started)])
        copy.start()
        self.started.append(copy)
        return copy

    def wait_all(self):
        for copy in self.started:
            copy.wait()


def slot_places(routes, experts, capacity):
    toks = routes.shape[1]
    r0 = routes[0:1, :]
    r1 = routes[1:2, :]
    expert = lax.broadcasted_iota(jnp.int32, (experts, toks), 0)
    named = jnp.where((expert == r0) | (expert == r1), 1.0, 0.0).astype(BF)
    row = lax.broadcasted_iota(jnp.int32, (toks, toks), 0)
    col = lax.broadcasted_iota(jnp.int32, (toks, toks), 1)
    earlier = jnp.where(row < col, 1.0, 0.0).astype(BF)
    before = dot(named, earlier)
    out = []
    for r in (r0, r1):
        slot = jnp.sum(jnp.where(expert == r, before, 0.0), axis=0, keepdims=True).astype(jnp.int32)
        out.append((r & 1, (r >> 1) * capacity + slot))
    return out


def matches(places, j, slots, toks):
    at = lax.broadcasted_iota(jnp.int32, (slots, toks), 0)
    return [at == jnp.where(which == j, place, -1) for which, place in places]


def on_device(tokens, out_cotangent, routes, gate_values, in_weight, out_weight):
    toks, quarter = tokens.shape
    groups = lax.axis_size("expert")
    n_local = in_weight.shape[0]
    experts = n_local * groups
    capacity = min(toks, 4 * toks // experts)
    slots = groups * capacity
    width, hidden = in_weight.shape[1:]
    n_chan = lax.axis_size("chan")
    half = slots // 2
    here = jnp.stack([lax.axis_index("dp"), lax.axis_index("chan")]).astype(jnp.int32)

    def shift(x, axis, by):
        n = lax.axis_size(axis)
        return lax.ppermute(x, axis, [(i, (i + by) % n) for i in range(n)])

    def pack_body(_, x_ref, dy_ref, routes_ref, gate_ref, *send_refs):
        places = slot_places(routes_ref[...], experts, capacity)
        gate = gate_ref[...].astype(F32)
        x = x_ref[...]
        dy = dy_ref[...]
        for j in range(n_local):
            m0, m1 = matches(places, j, slots, toks)
            pick = jnp.where(m0 | m1, 1.0, 0.0)
            gated = jnp.where(m0, gate[0:1, :], 0.0) + jnp.where(m1, gate[1:2, :], 0.0)
            send_refs[j][:, :quarter] = dot(pick.astype(BF), x).astype(BF)
            send_refs[j][:, quarter:] = dot(gated.astype(BF), dy).astype(BF)

    sends = call(
        pack_body,
        [here, tokens, out_cotangent, routes.T, gate_values.T],
        [((slots, 2 * quarter), BF)] * n_local,
        4 * n_local * slots * toks * quarter,
    )

    def exchange(x):
        return lax.all_to_all(
            x.reshape(groups, capacity, x.shape[1]), "expert", split_axis=0, concat_axis=0, tiled=True
        ).reshape(x.shape)

    def gather_parts(x):
        xa, xb = x[:half], x[half:]
        left_a = shift(xa, "chan", 1)
        right_b = shift(xb, "chan", -1)
        left_b = shift(xb, "chan", 1)
        right_a = shift(xa, "chan", -1)
        return [xa, xb, left_a, left_b, right_a, right_b, shift(left_a, "chan", 1), shift(right_b, "chan", -1)]

    def lay_out(copies, c, refs, first, full_ref):
        took = slice(first, first + quarter)
        if len(refs) == 1:
            return [
                copies.start(refs[0].at[k, :, took], full_ref.at[:, k * quarter : (k + 1) * quarter])
                for k in range(n_chan)
            ]
        started = []
        for n, k in enumerate((0, n_chan - 1, 1, 2)):
            cols = pl.ds(pl.multiple_of(((c + k) % n_chan) * quarter, quarter), quarter)
            started.append(copies.start(refs[2 * n].at[:, took], full_ref.at[:half, cols]))
            started.append(copies.start(refs[2 * n + 1].at[:, took], full_ref.at[half:, cols]))
        return started

    tile = 256
    tiles = hidden // tile
    n_dp = lax.axis_size("dp")

    def quarter_at(c, k):
        return pl.ds(pl.multiple_of(((c + k) % n_dp) * quarter, quarter), quarter)

    def pieces(rows, cols):
        return [((rows, cols), BF)] * n_dp

    def span(f):
        return slice(f * tile, (f + 1) * tile)

    def out_body(j, n_parts, here_ref, *refs):
        parts, w_ref, refs = refs[:n_parts], refs[n_parts], refs[n_parts + 1 :]
        xs_out, dys_out, act_out, slope_out, *piece_outs = refs[:8]
        xs, dys, act, slope, w, *piece_bufs = refs[8:-2]
        reads, writes = Copies(refs[-2]), Copies(refs[-1])
        x_here = lay_out(reads, here_ref[1], parts, 0, xs)
        w_here = [reads.start(w_ref.at[j, :, span(f)], w.at[:, span(f)]) for f in range(tiles)]
        dy_here = lay_out(reads, here_ref[1], parts, quarter, dys)
        for copy in x_here:
            copy.wait()
        for f in range(tiles):
            at = span(f)
            w_here[f].wait()
            pre = dot(xs[...], w[:, at])
            cdf = 0.5 * (1.0 + lax.erf(pre * (1.0 / math.sqrt(2.0))))
            dens = jnp.exp(-0.5 * pre * pre) * (1.0 / math.sqrt(2.0 * math.pi))
            value = pre * cdf
            slope[:, at] = (cdf + pre * dens).astype(BF)
            act[:, at] = value.astype(BF)
            act_t = value.T.astype(BF)
            if f == 0:
                for copy in dy_here:
                    copy.wait()
            for k in range(n_dp):
                piece_bufs[k][at, :] = dot(act_t, dys[:, quarter_at(here_ref[0], k)]).astype(BF)
                writes.start(piece_bufs[k].at[at, :], piece_outs[k].at[at, :])
            writes.start(act.at[:, at], act_out.at[:, at])
            writes.start(slope.at[:, at], slope_out.at[:, at])
        writes.start(xs, xs_out)
        writes.start(dys, dys_out)
        writes.wait_all()

    def in_body(j, n_rows, here_ref, dys_in, act_in, slope_in, xs_in, w_in, w_out, gate_ref, *refs):
        in_outs, row_outs, refs = refs[:4], refs[4 : 4 + n_rows], refs[4 + n_rows :]
        dys, act, slope, xs, w_i, w_o, grad, *bufs = refs[:-2]
        in_bufs, row_bufs = bufs[:4], bufs[4:]
        reads, writes = Copies(refs[-2]), Copies(refs[-1])
        dys_here = reads.start(dys_in, dys)
        tile_here = []
        for f in range(tiles):
            at = span(f)
            tile_here.append((
                reads.start(w_out.at[j, at, :], w_o.at[at, :]),
                reads.start(act_in.at[:, at], act.at[:, at]),
                reads.start(slope_in.at[:, at], slope.at[:, at]),
            ))
        xs_here = reads.start(xs_in, xs)
        w_here = reads.start(w_in.at[j], w_i)
        total = jnp.zeros((slots, 1), F32)
        dys_here.wait()
        for f in range(tiles):
            at = span(f)
            for copy in tile_here[f]:
                copy.wait()
            back = dot_t(dys[...], w_o[at, :])
            total += jnp.sum(act[:, at].astype(F32) * back, axis=1, keepdims=True)
            grad[:, at] = (back * slope[:, at].astype(F32)).astype(BF)
        gate_ref[...] = total
        xs_here.wait()
        for k in range(n_dp):
            x_t = xs[:, quarter_at(here_ref[0], k)].T
            for f in range(tiles):
                in_bufs[k][:, span(f)] = dot(x_t, grad[:, span(f)]).astype(BF)
            writes.start(in_bufs[k], in_outs[k])
        w_here.wait()
        for k in range(n_chan):
            at = quarter_at(here_ref[1], k) if n_rows > 1 else span(k)
            row_bufs[k][...] = dot_t(grad[...], w_i[at, :]).astype(BF)
            target = row_outs[k] if n_rows > 1 else row_outs[0].at[k * slots : (k + 1) * slots, :]
            writes.start(row_bufs[k], target)
        writes.wait_all()

    def add(a, b):
        return (a.astype(F32) + b.astype(F32)).astype(BF)

    def reduce_pieces(parts, axis, by):
        own, near, far = parts[0], parts[by % 4], parts[-by % 4]
        joined = add(near, shift(parts[2], axis, by))
        from_far = shift(far, axis, -by)
        from_near = shift(joined, axis, by)
        return (own.astype(F32) + from_near.astype(F32) + from_far.astype(F32)).astype(BF)

    received = []
    for j in range(n_local):
        sent = sends[j]
        if received:
            sent, received[-1] = lax.optimization_barrier((sent, received[-1]))
        received.append(exchange(sent))
    gates, rows_back, in_grads, out_grads = [], [], [], []
    for j in range(n_local):
        last = j + 1 == n_local
        if last:
            parts = [lax.all_gather(received[j], "chan", axis=0)]
        else:
            parts = gather_parts(received[j])
            *parts, received[j + 1] = lax.optimization_barrier((*parts, received[j + 1]))
        flops = 2 * slots * width * hidden
        wide = pltpu.VMEM((slots, width), BF)
        whole = pltpu.VMEM((width, hidden), BF)
        out_pieces = pieces(hidden, quarter)
        xs, dys, act, slope, *out_parts = call(
            functools.partial(out_body, j, len(parts)),
            [here, *parts, in_weight],
            [((slots, width), BF)] * 4 + out_pieces,
            2 * flops,
            len(parts) + 1,
            8,
            [wide, wide, wide, wide, whole]
            + [pltpu.VMEM(s, d) for s, d in out_pieces]
            + [pltpu.SemaphoreType.DMA((2 * max(len(parts), n_chan) + tiles,)), pltpu.SemaphoreType.DMA((6 * tiles + 2,))],
        )
        out_grads.append(reduce_pieces(out_parts, "dp", 1))
        in_pieces = pieces(quarter, hidden)
        row_pieces = pieces(slots, quarter)
        row_outs = row_pieces if last else [((n_chan * slots, quarter), BF)]
        gate_part, *more = call(
            functools.partial(in_body, j, len(row_outs)),
            [here, dys, act, slope, xs, in_weight, out_weight],
            [((slots, 1), F32)] + in_pieces + row_outs,
            3 * flops,
            6,
            4 + len(row_outs),
            [wide, wide, wide, wide, whole, whole, wide]
            + [pltpu.VMEM(s, d) for s, d in in_pieces + row_pieces]
            + [pltpu.SemaphoreType.DMA((3 * tiles + 3,)), pltpu.SemaphoreType.DMA((8,))],
        )
        in_parts, row_parts = more[:n_dp], more[n_dp:]
        in_grads.append(reduce_pieces(in_parts, "dp", -1))
        if last:
            row_sum = reduce_pieces(row_parts, "chan", -1)
        else:
            row_sum = lax.psum_scatter(row_parts[0], "chan", scatter_dimension=0, tiled=True)
        rows_back.append(exchange(row_sum))
        gates.append(gate_part.reshape(groups, capacity))

    gate_rows = jnp.concatenate(gates, axis=1)
    gate_rows = jnp.broadcast_to(gate_rows[:, None, :], (groups, n_chan, n_local * capacity))
    gate_rows = lax.all_to_all(
        gate_rows.reshape(groups * n_chan, n_local * capacity),
        ("expert", "chan"),
        split_axis=0,
        concat_axis=0,
        tiled=True,
    ).reshape(groups, n_chan, n_local, capacity)
    gate_rows = jnp.sum(gate_rows, axis=1).transpose(1, 0, 2).reshape(n_local, slots)

    def combine_body(_, routes_ref, gate_ref, sums_ref, *refs):
        rows_refs, (token_ref, gate_out_ref) = refs[:n_local], refs[n_local:]
        places = slot_places(routes_ref[...], experts, capacity)
        total = jnp.zeros((toks, quarter), F32)
        sums = [jnp.zeros((1, toks), F32), jnp.zeros((1, toks), F32)]
        for j in range(n_local):
            m = matches(places, j, slots, toks)
            pick = jnp.where(m[0] | m[1], 1.0, 0.0)
            total += dot(pick.T.astype(BF), rows_refs[j][...])
            for k in range(2):
                mask = jnp.where(m[k], 1.0, 0.0)
                sums[k] += jnp.dot(sums_ref[j : j + 1, :], mask, preferred_element_type=F32, precision=lax.Precision.HIGHEST)
        token_ref[...] = total.astype(BF)
        gate = gate_ref[...].astype(F32)
        for k in range(2):
            gate_out_ref[k : k + 1, :] = (sums[k] / gate[k : k + 1, :]).astype(BF)

    token_grads, gate_grads = call(
        combine_body,
        [here, routes.T, gate_values.T, gate_rows, *rows_back],
        [((toks, quarter), BF), (gate_values.shape[::-1], BF)],
        2 * n_local * slots * toks * quarter,
    )
    gate_grads = gate_grads.T
    return (token_grads, gate_grads, jnp.stack(in_grads), jnp.stack(out_grads))


def solution(mesh):
    placed = (
        P(("dp", "expert"), "chan"),
        P(("dp", "expert"), "chan"),
        P(("dp", "expert"), None),
        P(("dp", "expert"), None),
        P("expert", None, "chan"),
        P("expert", "chan", None),
    )
    return jax.shard_map(
        on_device,
        mesh=mesh,
        in_specs=placed,
        out_specs=(
            P(("dp", "expert"), "chan"),
            P(("dp", "expert"), None),
            P("expert", "dp", "chan"),
            P("expert", "chan", "dp"),
        ),
        check_vma=False,
    )
```

```python
import functools
import math

import jax
import jax.numpy as jnp
from jax import lax
from jax.experimental import pallas as pl
from jax.experimental.pallas import tpu as pltpu
from jax.sharding import PartitionSpec as P

BF = jnp.bfloat16
F32 = jnp.float32
VMEM_BYTES = 60 * 1024 * 1024


def dot(a, b):
    return jnp.dot(a, b, preferred_element_type=F32)


def dot_t(a, b):
    return lax.dot_general(a, b, (((1,), (1,)), ((), ())), preferred_element_type=F32)


def call(body, ins, outs, flops, far_ins=0, far_outs=0, scratch=()):
    far = pl.BlockSpec(memory_space=pl.ANY)

    def specs(shapes, n_far):
        near = len(shapes) - n_far
        return [pl.BlockSpec(s, lambda i, n=len(s): (0,) * n) for s in shapes[:near]] + [far] * n_far

    moved = sum(x.size * x.dtype.itemsize for x in ins) + sum(
        math.prod(s) * jnp.dtype(d).itemsize for s, d in outs
    )
    return pl.pallas_call(
        body,
        grid=(1,),
        in_specs=[pl.BlockSpec(memory_space=pltpu.SMEM)] + specs([x.shape for x in ins[1:]], far_ins),
        out_specs=specs([s for s, _ in outs], far_outs),
        out_shape=[jax.ShapeDtypeStruct(s, d) for s, d in outs],
        scratch_shapes=scratch,
        compiler_params=pltpu.CompilerParams(vmem_limit_bytes=VMEM_BYTES),
        cost_estimate=pl.CostEstimate(flops=flops // 16, bytes_accessed=moved // 16, transcendentals=0),
    )(*ins)


class Copies:
    def __init__(self, sems):
        self.sems = sems
        self.started = []

    def start(self, source, target):
        copy = pltpu.make_async_copy(source, target, self.sems.at[len(self.started)])
        copy.start()
        self.started.append(copy)
        return copy

    def wait_all(self):
        for copy in self.started:
            copy.wait()


def slot_places(routes, experts, capacity):
    toks = routes.shape[1]
    r0 = routes[0:1, :]
    r1 = routes[1:2, :]
    expert = lax.broadcasted_iota(jnp.int32, (experts, toks), 0)
    named = jnp.where((expert == r0) | (expert == r1), 1.0, 0.0).astype(BF)
    row = lax.broadcasted_iota(jnp.int32, (toks, toks), 0)
    col = lax.broadcasted_iota(jnp.int32, (toks, toks), 1)
    earlier = jnp.where(row < col, 1.0, 0.0).astype(BF)
    before = dot(named, earlier)
    out = []
    for r in (r0, r1):
        slot = jnp.sum(jnp.where(expert == r, before, 0.0), axis=0, keepdims=True).astype(jnp.int32)
        out.append((r & 1, (r >> 1) * capacity + slot))
    return out


def matches(places, j, slots, toks):
    at = lax.broadcasted_iota(jnp.int32, (slots, toks), 0)
    return [at == jnp.where(which == j, place, -1) for which, place in places]


def on_device(tokens, out_cotangent, routes, gate_values, in_weight, out_weight):
    toks, quarter = tokens.shape
    groups = lax.axis_size("expert")
    n_local = in_weight.shape[0]
    experts = n_local * groups
    capacity = min(toks, 4 * toks // experts)
    slots = groups * capacity
    width, hidden = in_weight.shape[1:]
    n_chan = lax.axis_size("chan")
    half = slots // 2
    here = jnp.stack([lax.axis_index("dp"), lax.axis_index("chan")]).astype(jnp.int32)

    def shift(x, axis, by):
        n = lax.axis_size(axis)
        return lax.ppermute(x, axis, [(i, (i + by) % n) for i in range(n)])

    def pack_body(_, x_ref, dy_ref, routes_ref, gate_ref, *send_refs):
        places = slot_places(routes_ref[...], experts, capacity)
        gate = gate_ref[...].astype(F32)
        x = x_ref[...]
        dy = dy_ref[...]
        for j in range(n_local):
            m0, m1 = matches(places, j, slots, toks)
            pick = jnp.where(m0 | m1, 1.0, 0.0)
            gated = jnp.where(m0, gate[0:1, :], 0.0) + jnp.where(m1, gate[1:2, :], 0.0)
            send_refs[j][:, :quarter] = dot(pick.astype(BF), x).astype(BF)
            send_refs[j][:, quarter:] = dot(gated.astype(BF), dy).astype(BF)

    sends = call(
        pack_body,
        [here, tokens, out_cotangent, routes.T, gate_values.T],
        [((slots, 2 * quarter), BF)] * n_local,
        4 * n_local * slots * toks * quarter,
    )

    def exchange(x):
        return lax.all_to_all(
            x.reshape(groups, capacity, x.shape[1]), "expert", split_axis=0, concat_axis=0, tiled=True
        ).reshape(x.shape)

    def gather_parts(x, in_halves):
        xa, xb = x[:half], x[half:]
        if in_halves:
            left_a = shift(xa, "chan", 1)
            right_b = shift(xb, "chan", -1)
            near = [xa, xb, left_a, shift(xb, "chan", 1), shift(xa, "chan", -1), right_b]
        else:
            left = shift(x, "chan", 1)
            right = shift(x, "chan", -1)
            left_a, right_b = left[:half], right[half:]
            near = [x, left, right]
        return [*near, shift(left_a, "chan", 1), shift(right_b, "chan", -1)]

    def lay_out(copies, c, refs, first, full_ref):
        took = slice(first, first + quarter)
        started = []
        at = 0
        for k in (0, n_chan - 1, 1, 2):
            cols = pl.ds(pl.multiple_of(((c + k) % n_chan) * quarter, quarter), quarter)
            row = 0
            while row < slots:
                rows = refs[at].shape[0]
                started.append(copies.start(refs[at].at[:, took], full_ref.at[row : row + rows, cols]))
                row += rows
                at += 1
        return started

    tile = 512
    tiles = hidden // tile
    n_dp = lax.axis_size("dp")

    def quarter_at(c, k):
        return pl.ds(pl.multiple_of(((c + k) % n_dp) * quarter, quarter), quarter)

    def pieces(rows, cols):
        return [((rows, cols), BF)] * n_dp

    def span(f):
        return slice(f * tile, (f + 1) * tile)

    def expert_body(j, n_parts, here_ref, *refs):
        parts, (w_in, w_out, gate_ref), refs = refs[:n_parts], refs[n_parts : n_parts + 3], refs[n_parts + 3 :]
        out_outs, in_outs, row_outs, refs = refs[:4], refs[4:8], refs[8:12], refs[12:]
        xs, dys, act, slope, grad, w_i, w_o, *bufs = refs[:-2]
        out_bufs, in_bufs, row_bufs = bufs[:4], bufs[4:8], bufs[8:]
        reads, writes = Copies(refs[-2]), Copies(refs[-1])
        x_here = lay_out(reads, here_ref[1], parts, 0, xs)
        wi_here = [reads.start(w_in.at[j, :, span(f)], w_i.at[:, span(f)]) for f in range(tiles)]
        dy_here = lay_out(reads, here_ref[1], parts, quarter, dys)
        wo_here = reads.start(w_out.at[j], w_o)
        for copy in x_here:
            copy.wait()
        for f in range(tiles):
            at = span(f)
            wi_here[f].wait()
            pre = dot(xs[...], w_i[:, at])
            cdf = 0.5 * (1.0 + lax.erf(pre * (1.0 / math.sqrt(2.0))))
            dens = jnp.exp(-0.5 * pre * pre) * (1.0 / math.sqrt(2.0 * math.pi))
            value = (pre * cdf).astype(BF)
            slope[:, at] = (cdf + pre * dens).astype(BF)
            act[:, at] = value
            act_t = value.T
            if f == 0:
                for copy in dy_here:
                    copy.wait()
            for k in range(n_dp):
                out_bufs[k][at, :] = dot(act_t, dys[:, quarter_at(here_ref[0], k)]).astype(BF)
        for k in range(n_dp):
            writes.start(out_bufs[k], out_outs[k])
        wo_here.wait()
        total = jnp.zeros((slots, 1), F32)
        for f in range(tiles):
            at = span(f)
            back = dot_t(dys[...], w_o[at, :])
            total += jnp.sum(act[:, at].astype(F32) * back, axis=1, keepdims=True)
            grad[:, at] = (back * slope[:, at].astype(F32)).astype(BF)
        gate_ref[...] = total
        for k in (2, 1, 3, 0):
            x_t = xs[:, quarter_at(here_ref[0], k)].T
            for f in range(tiles):
                in_bufs[k][:, span(f)] = dot(x_t, grad[:, span(f)]).astype(BF)
            writes.start(in_bufs[k], in_outs[k])
        for k in (2, 1, 3, 0):
            row_bufs[k][...] = dot_t(grad[...], w_i[quarter_at(here_ref[1], k), :]).astype(BF)
            writes.start(row_bufs[k], row_outs[k])
        writes.wait_all()

    def add(a, b):
        return (a.astype(F32) + b.astype(F32)).astype(BF)

    def reduce_end(parts, got, axis, by):
        own, near, far = parts[0], parts[by % 4], parts[-by % 4]
        from_far = shift(far, axis, -by)
        return [own, shift(add(near, got), axis, by), from_far]

    def total(terms):
        return sum(t.astype(F32) for t in terms).astype(BF)

    received = []
    for j in range(n_local):
        sent = sends[j]
        if received:
            sent, received[-1] = lax.optimization_barrier((sent, received[-1]))
        received.append(exchange(sent))
    flops = 2 * slots * width * hidden
    wide = pltpu.VMEM((slots, width), BF)
    whole = pltpu.VMEM((width, hidden), BF)
    results = pieces(hidden, quarter) + pieces(quarter, hidden) + pieces(slots, quarter)
    gates, made, arrived, out_terms, in_terms = [], [], [], [], []
    for j in range(n_local):
        parts = gather_parts(received[j], j == 0)
        if j + 1 < n_local:
            *parts, received[j + 1] = lax.optimization_barrier((*parts, received[j + 1]))
        if j:
            *parts, arrived[0], arrived[1] = lax.optimization_barrier((*parts, *arrived))
            out_terms.append(reduce_end(made[-1][:n_dp], arrived[0], "dp", 1))
            in_terms.append(reduce_end(made[-1][n_dp : 2 * n_dp], arrived[1], "dp", -1))
        gate_part, *results_j = call(
            functools.partial(expert_body, j, len(parts)),
            [here, *parts, in_weight, out_weight],
            [((slots, 1), F32)] + results,
            5 * flops,
            len(parts) + 2,
            len(results),
            [wide] * 5
            + [whole] * 2
            + [pltpu.VMEM(s, d) for s, d in results]
            + [pltpu.SemaphoreType.DMA((2 * len(parts) + tiles + 1,)), pltpu.SemaphoreType.DMA((len(results),))],
        )
        made.append(results_j)
        gates.append(gate_part)
        arrived = [shift(results_j[2], "dp", 1), shift(results_j[n_dp + 2], "dp", -1)]
    out_terms.append(reduce_end(made[-1][:n_dp], arrived[0], "dp", 1))
    in_terms.append(reduce_end(made[-1][n_dp : 2 * n_dp], arrived[1], "dp", -1))

    row_parts = [m[2 * n_dp :] for m in made]
    row_parts, gates, out_terms[0], in_terms[0] = lax.optimization_barrier(
        (row_parts, gates, out_terms[0], in_terms[0])
    )
    rows_back = []
    for j in range(n_local):
        by = 1 - 2 * (j % 2)
        rows_back.append(exchange(total(reduce_end(row_parts[j], shift(row_parts[j][2], "chan", by), "chan", by))))
    out_grads = [total(t) for t in out_terms]
    in_grads = [total(t) for t in in_terms]
    gates = [g.reshape(groups, capacity) for g in gates]

    gate_rows = jnp.concatenate(gates, axis=1)
    gate_rows = jnp.broadcast_to(gate_rows[:, None, :], (groups, n_chan, n_local * capacity))
    gate_rows = lax.all_to_all(
        gate_rows.reshape(groups * n_chan, n_local * capacity),
        ("expert", "chan"),
        split_axis=0,
        concat_axis=0,
        tiled=True,
    ).reshape(groups, n_chan, n_local, capacity)
    gate_rows = jnp.sum(gate_rows, axis=1).transpose(1, 0, 2).reshape(n_local, slots)

    def combine_body(_, routes_ref, gate_ref, sums_ref, *refs):
        rows_refs, (token_ref, gate_out_ref) = refs[:n_local], refs[n_local:]
        places = slot_places(routes_ref[...], experts, capacity)
        total = jnp.zeros((toks, quarter), F32)
        sums = [jnp.zeros((1, toks), F32), jnp.zeros((1, toks), F32)]
        for j in range(n_local):
            m = matches(places, j, slots, toks)
            pick = jnp.where(m[0] | m[1], 1.0, 0.0)
            total += dot(pick.T.astype(BF), rows_refs[j][...])
            for k in range(2):
                mask = jnp.where(m[k], 1.0, 0.0)
                sums[k] += jnp.dot(sums_ref[j : j + 1, :], mask, preferred_element_type=F32, precision=lax.Precision.HIGHEST)
        token_ref[...] = total.astype(BF)
        gate = gate_ref[...].astype(F32)
        for k in range(2):
            gate_out_ref[k : k + 1, :] = (sums[k] / gate[k : k + 1, :]).astype(BF)

    token_grads, gate_grads = call(
        combine_body,
        [here, routes.T, gate_values.T, gate_rows, *rows_back],
        [((toks, quarter), BF), (gate_values.shape[::-1], BF)],
        2 * n_local * slots * toks * quarter,
    )
    gate_grads = gate_grads.T
    return (token_grads, gate_grads, jnp.stack(in_grads), jnp.stack(out_grads))


def solution(mesh):
    placed = (
        P(("dp", "expert"), "chan"),
        P(("dp", "expert"), "chan"),
        P(("dp", "expert"), None),
        P(("dp", "expert"), None),
        P("expert", None, "chan"),
        P("expert", "chan", None),
    )
    return jax.shard_map(
        on_device,
        mesh=mesh,
        in_specs=placed,
        out_specs=(
            P(("dp", "expert"), "chan"),
            P(("dp", "expert"), None),
            P("expert", "dp", "chan"),
            P("expert", "chan", "dp"),
        ),
        check_vma=False,
    )
```

```python
import functools
import math

import jax
import jax.numpy as jnp
from jax import lax
from jax.experimental import pallas as pl
from jax.experimental.pallas import tpu as pltpu
from jax.sharding import PartitionSpec as P

BF = jnp.bfloat16
F32 = jnp.float32
VMEM_BYTES = 60 * 1024 * 1024


def dot(a, b):
    return jnp.dot(a, b, preferred_element_type=F32)


def dot_t(a, b):
    return lax.dot_general(a, b, (((1,), (1,)), ((), ())), preferred_element_type=F32)


def call(body, ins, outs, flops, far_ins=0, far_outs=0, scratch=()):
    far = pl.BlockSpec(memory_space=pl.ANY)

    def specs(shapes, n_far):
        near = len(shapes) - n_far
        return [pl.BlockSpec(s, lambda i, n=len(s): (0,) * n) for s in shapes[:near]] + [far] * n_far

    moved = sum(x.size * x.dtype.itemsize for x in ins) + sum(
        math.prod(s) * jnp.dtype(d).itemsize for s, d in outs
    )
    return pl.pallas_call(
        body,
        grid=(1,),
        in_specs=[pl.BlockSpec(memory_space=pltpu.SMEM)] + specs([x.shape for x in ins[1:]], far_ins),
        out_specs=specs([s for s, _ in outs], far_outs),
        out_shape=[jax.ShapeDtypeStruct(s, d) for s, d in outs],
        scratch_shapes=scratch,
        compiler_params=pltpu.CompilerParams(vmem_limit_bytes=VMEM_BYTES),
        cost_estimate=pl.CostEstimate(flops=flops // 16, bytes_accessed=moved // 16, transcendentals=0),
    )(*ins)


class Copies:
    def __init__(self, sems):
        self.sems = sems
        self.started = []

    def start(self, source, target):
        copy = pltpu.make_async_copy(source, target, self.sems.at[len(self.started)])
        copy.start()
        self.started.append(copy)
        return copy

    def wait_all(self):
        for copy in self.started:
            copy.wait()


def slot_places(routes, experts, capacity):
    toks = routes.shape[1]
    r0 = routes[0:1, :]
    r1 = routes[1:2, :]
    expert = lax.broadcasted_iota(jnp.int32, (experts, toks), 0)
    named = jnp.where((expert == r0) | (expert == r1), 1.0, 0.0).astype(BF)
    row = lax.broadcasted_iota(jnp.int32, (toks, toks), 0)
    col = lax.broadcasted_iota(jnp.int32, (toks, toks), 1)
    earlier = jnp.where(row < col, 1.0, 0.0).astype(BF)
    before = dot(named, earlier)
    out = []
    for r in (r0, r1):
        slot = jnp.sum(jnp.where(expert == r, before, 0.0), axis=0, keepdims=True).astype(jnp.int32)
        out.append((r & 1, (r >> 1) * capacity + slot))
    return out


def matches(places, j, slots, toks):
    at = lax.broadcasted_iota(jnp.int32, (slots, toks), 0)
    return [at == jnp.where(which == j, place, -1) for which, place in places]


def on_device(tokens, out_cotangent, routes, gate_values, in_weight, out_weight):
    toks, quarter = tokens.shape
    groups = lax.axis_size("expert")
    n_local = in_weight.shape[0]
    experts = n_local * groups
    capacity = min(toks, 4 * toks // experts)
    slots = groups * capacity
    width, hidden = in_weight.shape[1:]
    n_chan = lax.axis_size("chan")
    half = slots // 2
    here = jnp.stack([lax.axis_index("dp"), lax.axis_index("chan")]).astype(jnp.int32)

    def shift(x, axis, by):
        n = lax.axis_size(axis)
        return lax.ppermute(x, axis, [(i, (i + by) % n) for i in range(n)])

    def pack_body(_, x_ref, dy_ref, routes_ref, gate_ref, *send_refs):
        places = slot_places(routes_ref[...], experts, capacity)
        gate = gate_ref[...].astype(F32)
        x = x_ref[...]
        dy = dy_ref[...]
        for j in range(n_local):
            m0, m1 = matches(places, j, slots, toks)
            pick = jnp.where(m0 | m1, 1.0, 0.0)
            gated = jnp.where(m0, gate[0:1, :], 0.0) + jnp.where(m1, gate[1:2, :], 0.0)
            send_refs[j][:, :quarter] = dot(pick.astype(BF), x).astype(BF)
            send_refs[j][:, quarter:] = dot(gated.astype(BF), dy).astype(BF)

    sends = call(
        pack_body,
        [here, tokens, out_cotangent, routes.T, gate_values.T],
        [((slots, 2 * quarter), BF)] * n_local,
        4 * n_local * slots * toks * quarter,
    )

    def exchange(x):
        return lax.all_to_all(
            x.reshape(groups, x.shape[0] // groups, x.shape[1]), "expert", split_axis=0, concat_axis=0, tiled=True
        ).reshape(x.shape)

    def gather_parts(x, in_halves):
        xa, xb = x[:half], x[half:]
        if in_halves:
            left_a = shift(xa, "chan", 1)
            right_b = shift(xb, "chan", -1)
            near = [xa, xb, left_a, shift(xb, "chan", 1), shift(xa, "chan", -1), right_b]
        else:
            left = shift(x, "chan", 1)
            right = shift(x, "chan", -1)
            left_a, right_b = left[:half], right[half:]
            near = [x, left, right]
        return [*near, shift(left_a, "chan", 1), shift(right_b, "chan", -1)]

    def lay_out(copies, c, refs, first, full_ref):
        took = slice(first, first + quarter)
        started = []
        at = 0
        for k in (0, n_chan - 1, 1, 2):
            cols = pl.ds(pl.multiple_of(((c + k) % n_chan) * quarter, quarter), quarter)
            row = 0
            while row < slots:
                rows = refs[at].shape[0]
                started.append(copies.start(refs[at].at[:, took], full_ref.at[row : row + rows, cols]))
                row += rows
                at += 1
        return started

    tile = 512
    tiles = hidden // tile
    n_dp = lax.axis_size("dp")

    def quarter_at(c, k):
        return pl.ds(pl.multiple_of(((c + k) % n_dp) * quarter, quarter), quarter)

    def pieces(rows, cols):
        return [((rows, cols), BF)] * n_dp

    def span(f):
        return slice(f * tile, (f + 1) * tile)

    def expert_body(j, n_parts, here_ref, *refs):
        parts, (w_in, w_out, gate_ref), refs = refs[:n_parts], refs[n_parts : n_parts + 3], refs[n_parts + 3 :]
        out_outs, in_outs, refs = refs[:4], refs[4:8], refs[8:]
        n_rows = len(refs) - 21
        row_outs, refs = refs[:n_rows], refs[n_rows:]
        xs, dys, act, slope, grad, w_i, w_o, *bufs = refs[:-2]
        out_bufs, in_bufs, row_bufs = bufs[:4], bufs[4:8], bufs[8:]
        reads, writes = Copies(refs[-2]), Copies(refs[-1])
        x_here = lay_out(reads, here_ref[1], parts, 0, xs)
        wi_here = [reads.start(w_in.at[j, :, span(f)], w_i.at[:, span(f)]) for f in range(tiles)]
        dy_here = lay_out(reads, here_ref[1], parts, quarter, dys)
        wo_here = reads.start(w_out.at[j], w_o)
        for copy in x_here:
            copy.wait()
        for f in range(tiles):
            at = span(f)
            wi_here[f].wait()
            pre = dot(xs[...], w_i[:, at])
            cdf = 0.5 * (1.0 + lax.erf(pre * (1.0 / math.sqrt(2.0))))
            dens = jnp.exp(-0.5 * pre * pre) * (1.0 / math.sqrt(2.0 * math.pi))
            value = (pre * cdf).astype(BF)
            slope[:, at] = (cdf + pre * dens).astype(BF)
            act[:, at] = value
            act_t = value.T
            if f == 0:
                for copy in dy_here:
                    copy.wait()
            for k in range(n_dp):
                out_bufs[k][at, :] = dot(act_t, dys[:, quarter_at(here_ref[0], k)]).astype(BF)
        for k in range(n_dp):
            writes.start(out_bufs[k], out_outs[k])
        wo_here.wait()
        total = jnp.zeros((slots, 1), F32)
        for f in range(tiles):
            at = span(f)
            back = dot_t(dys[...], w_o[at, :])
            total += jnp.sum(act[:, at].astype(F32) * back, axis=1, keepdims=True)
            grad[:, at] = (back * slope[:, at].astype(F32)).astype(BF)
        gate_ref[...] = total
        for k in (2, 1, 3, 0):
            x_t = xs[:, quarter_at(here_ref[0], k)].T
            for f in range(tiles):
                in_bufs[k][:, span(f)] = dot(x_t, grad[:, span(f)]).astype(BF)
            writes.start(in_bufs[k], in_outs[k])
        for k in (2, 1, 3, 0):
            row_bufs[k][...] = dot_t(grad[...], w_i[quarter_at(here_ref[1], k), :]).astype(BF)
            writes.start(row_bufs[k], row_outs[k] if n_rows > 1 else row_outs[0].at[(here_ref[1] + k) % n_chan])
        writes.wait_all()

    def add(a, b):
        return (a.astype(F32) + b.astype(F32)).astype(BF)

    def reduce_start(parts, axis, by):
        return [shift(parts[2], axis, by), shift(parts[-by % 4], axis, -by)]

    def reduce_end(parts, arrived, axis, by):
        return [parts[0], shift(add(parts[by % 4], arrived[0]), axis, by), arrived[1]]

    def total(terms):
        return sum(t.astype(F32) for t in terms).astype(BF)

    received = []
    for j in range(n_local):
        sent = sends[j]
        if received:
            sent, received[-1] = lax.optimization_barrier((sent, received[-1]))
        received.append(exchange(sent))
    flops = 2 * slots * width * hidden
    wide = pltpu.VMEM((slots, width), BF)
    whole = pltpu.VMEM((width, hidden), BF)
    weight_pieces = pieces(hidden, quarter) + pieces(quarter, hidden)
    row_pieces = pieces(slots, quarter)
    gates, made, arrived, out_terms, in_terms = [], [], [], [], []
    for j in range(n_local):
        parts = gather_parts(received[j], j == 0)
        if j + 1 < n_local:
            *parts, received[j + 1] = lax.optimization_barrier((*parts, received[j + 1]))
        if j:
            stacked = lax.all_to_all(made[-1][-1], "chan", split_axis=0, concat_axis=0, tiled=True)
            parts, arrived = lax.optimization_barrier((parts, arrived))
            back_terms = stacked
            out_terms.append(reduce_end(made[-1][:n_dp], arrived[0], "dp", 1))
            in_terms.append(reduce_end(made[-1][n_dp : 2 * n_dp], arrived[1], "dp", -1))
        results = weight_pieces + (row_pieces if j else [((n_chan, slots, quarter), BF)])
        gate_part, *results_j = call(
            functools.partial(expert_body, j, len(parts)),
            [here, *parts, in_weight, out_weight],
            [((slots, 1), F32)] + results,
            5 * flops,
            len(parts) + 2,
            len(results),
            [wide] * 5
            + [whole] * 2
            + [pltpu.VMEM(s, d) for s, d in weight_pieces + row_pieces]
            + [pltpu.SemaphoreType.DMA((2 * len(parts) + tiles + 1,)), pltpu.SemaphoreType.DMA((3 * n_dp,))],
        )
        made.append(results_j)
        gates.append(gate_part)
        arrived = [reduce_start(results_j[:n_dp], "dp", 1), reduce_start(results_j[n_dp : 2 * n_dp], "dp", -1)]
    out_terms.append(reduce_end(made[-1][:n_dp], arrived[0], "dp", 1))
    in_terms.append(reduce_end(made[-1][n_dp : 2 * n_dp], arrived[1], "dp", -1))

    row_parts = made[-1][2 * n_dp :]
    row_parts, out_terms[0], in_terms[0], gates = lax.optimization_barrier((row_parts, out_terms[0], in_terms[0], gates))
    row_arrived = reduce_start(row_parts, "chan", 1)
    row_sums = [total([back_terms[c] for c in range(n_chan)]), total(reduce_end(row_parts, row_arrived, "chan", 1))]
    back = jnp.concatenate([r.reshape(groups, capacity, quarter) for r in row_sums], axis=1)
    rows_back = exchange(back.reshape(n_local * slots, quarter))
    out_grads = [total(t) for t in out_terms]
    in_grads = [total(t) for t in in_terms]
    gate_rows = jnp.concatenate([g.reshape(groups, capacity) for g in gates], axis=1)
    gate_rows = jnp.broadcast_to(gate_rows[:, None, :], (groups, n_chan, n_local * capacity))
    gate_rows = lax.all_to_all(
        gate_rows.reshape(groups * n_chan, n_local * capacity),
        ("expert", "chan"),
        split_axis=0,
        concat_axis=0,
        tiled=True,
    ).reshape(groups, n_chan, n_local * capacity)
    gate_rows = jnp.sum(gate_rows, axis=1).reshape(1, n_local * slots)

    def combine_body(_, routes_ref, gate_ref, sums_ref, rows_ref, token_ref, gate_out_ref):
        places = slot_places(routes_ref[...], experts, capacity)
        at = lax.broadcasted_iota(jnp.int32, (n_local * slots, toks), 0)
        hits = []
        for which, place in places:
            group = lax.div(place, capacity)
            hits.append(at == place + (group * (n_local - 1) + which) * capacity)
        pick = jnp.where(hits[0] | hits[1], 1.0, 0.0)
        token_ref[...] = dot(pick.T.astype(BF), rows_ref[...]).astype(BF)
        gate = gate_ref[...].astype(F32)
        for k in range(2):
            mask = jnp.where(hits[k], 1.0, 0.0)
            found = jnp.dot(sums_ref[...], mask, preferred_element_type=F32, precision=lax.Precision.HIGHEST)
            gate_out_ref[k : k + 1, :] = (found / gate[k : k + 1, :]).astype(BF)

    token_grads, gate_grads = call(
        combine_body,
        [here, routes.T, gate_values.T, gate_rows, rows_back],
        [((toks, quarter), BF), (gate_values.shape[::-1], BF)],
        2 * n_local * slots * toks * quarter,
    )
    gate_grads = gate_grads.T
    return (token_grads, gate_grads, jnp.stack(in_grads), jnp.stack(out_grads))


def solution(mesh):
    placed = (
        P(("dp", "expert"), "chan"),
        P(("dp", "expert"), "chan"),
        P(("dp", "expert"), None),
        P(("dp", "expert"), None),
        P("expert", None, "chan"),
        P("expert", "chan", None),
    )
    return jax.shard_map(
        on_device,
        mesh=mesh,
        in_specs=placed,
        out_specs=(
            P(("dp", "expert"), "chan"),
            P(("dp", "expert"), None),
            P("expert", "dp", "chan"),
            P("expert", "chan", "dp"),
        ),
        check_vma=False,
    )
```

```python
import functools
import math

import jax
import jax.numpy as jnp
from jax import lax
from jax.experimental import pallas as pl
from jax.experimental.pallas import tpu as pltpu
from jax.sharding import PartitionSpec as P

BF = jnp.bfloat16
F32 = jnp.float32
VMEM_BYTES = 60 * 1024 * 1024


def dot(a, b):
    return jnp.dot(a, b, preferred_element_type=F32)


def dot_t(a, b):
    return lax.dot_general(a, b, (((1,), (1,)), ((), ())), preferred_element_type=F32)


def call(body, ins, outs, flops, far_ins=0, far_outs=0, scratch=()):
    far = pl.BlockSpec(memory_space=pl.ANY)

    def specs(shapes, n_far):
        near = len(shapes) - n_far
        return [pl.BlockSpec(s, lambda i, n=len(s): (0,) * n) for s in shapes[:near]] + [far] * n_far

    moved = sum(x.size * x.dtype.itemsize for x in ins) + sum(
        math.prod(s) * jnp.dtype(d).itemsize for s, d in outs
    )
    return pl.pallas_call(
        body,
        grid=(1,),
        in_specs=[pl.BlockSpec(memory_space=pltpu.SMEM)] + specs([x.shape for x in ins[1:]], far_ins),
        out_specs=specs([s for s, _ in outs], far_outs),
        out_shape=[jax.ShapeDtypeStruct(s, d) for s, d in outs],
        scratch_shapes=scratch,
        compiler_params=pltpu.CompilerParams(vmem_limit_bytes=VMEM_BYTES),
        cost_estimate=pl.CostEstimate(flops=flops // 16, bytes_accessed=moved // 16, transcendentals=0),
    )(*ins)


class Copies:
    def __init__(self, sems):
        self.sems = sems
        self.started = []

    def start(self, source, target):
        copy = pltpu.make_async_copy(source, target, self.sems.at[len(self.started)])
        copy.start()
        self.started.append(copy)
        return copy

    def wait_all(self):
        for copy in self.started:
            copy.wait()


def slot_places(routes, experts, capacity):
    toks = routes.shape[1]
    r0 = routes[0:1, :]
    r1 = routes[1:2, :]
    expert = lax.broadcasted_iota(jnp.int32, (experts, toks), 0)
    named = jnp.where((expert == r0) | (expert == r1), 1.0, 0.0).astype(BF)
    row = lax.broadcasted_iota(jnp.int32, (toks, toks), 0)
    col = lax.broadcasted_iota(jnp.int32, (toks, toks), 1)
    earlier = jnp.where(row < col, 1.0, 0.0).astype(BF)
    before = dot(named, earlier)
    out = []
    for r in (r0, r1):
        slot = jnp.sum(jnp.where(expert == r, before, 0.0), axis=0, keepdims=True).astype(jnp.int32)
        out.append((r & 1, (r >> 1) * capacity + slot))
    return out


def matches(places, j, slots, toks):
    at = lax.broadcasted_iota(jnp.int32, (slots, toks), 0)
    return [at == jnp.where(which == j, place, -1) for which, place in places]


def on_device(tokens, out_cotangent, routes, gate_values, in_weight, out_weight):
    toks, quarter = tokens.shape
    groups = lax.axis_size("expert")
    n_local = in_weight.shape[0]
    experts = n_local * groups
    capacity = min(toks, 4 * toks // experts)
    slots = groups * capacity
    width, hidden = in_weight.shape[1:]
    n_chan = lax.axis_size("chan")
    half = slots // 2
    here = jnp.stack([lax.axis_index("dp"), lax.axis_index("chan")]).astype(jnp.int32)

    def shift(x, axis, by):
        n = lax.axis_size(axis)
        return lax.ppermute(x, axis, [(i, (i + by) % n) for i in range(n)])

    def pack_body(_, x_ref, dy_ref, routes_ref, gate_ref, *send_refs):
        places = slot_places(routes_ref[...], experts, capacity)
        gate = gate_ref[...].astype(F32)
        x = x_ref[...]
        dy = dy_ref[...]
        for j in range(n_local):
            m0, m1 = matches(places, j, slots, toks)
            pick = jnp.where(m0 | m1, 1.0, 0.0)
            gated = jnp.where(m0, gate[0:1, :], 0.0) + jnp.where(m1, gate[1:2, :], 0.0)
            send_refs[j][:, :quarter] = dot(pick.astype(BF), x).astype(BF)
            send_refs[j][:, quarter:] = dot(gated.astype(BF), dy).astype(BF)

    sends = call(
        pack_body,
        [here, tokens, out_cotangent, routes.T, gate_values.T],
        [((slots, 2 * quarter), BF)] * n_local,
        4 * n_local * slots * toks * quarter,
    )

    def exchange(x):
        return lax.all_to_all(
            x.reshape(groups, x.shape[0] // groups, x.shape[1]), "expert", split_axis=0, concat_axis=0, tiled=True
        ).reshape(x.shape)

    def gather_parts(x, in_halves):
        xa, xb = x[:half], x[half:]
        if in_halves:
            left_a = shift(xa, "chan", 1)
            right_b = shift(xb, "chan", -1)
            near = [xa, xb, left_a, shift(xb, "chan", 1), shift(xa, "chan", -1), right_b]
        else:
            left = shift(x, "chan", 1)
            right = shift(x, "chan", -1)
            left_a, right_b = left[:half], right[half:]
            near = [x, left, right]
        return [*near, shift(left_a, "chan", 1), shift(right_b, "chan", -1)]

    def lay_out(copies, c, refs, first, full_ref):
        took = slice(first, first + quarter)
        started = []
        at = 0
        for k in (0, n_chan - 1, 1, 2):
            cols = pl.ds(pl.multiple_of(((c + k) % n_chan) * quarter, quarter), quarter)
            row = 0
            while row < slots:
                rows = refs[at].shape[0]
                started.append(copies.start(refs[at].at[:, took], full_ref.at[row : row + rows, cols]))
                row += rows
                at += 1
        return started

    tile = 512
    tiles = hidden // tile
    n_dp = lax.axis_size("dp")

    def quarter_at(c, k):
        return pl.ds(pl.multiple_of(((c + k) % n_dp) * quarter, quarter), quarter)

    def pieces(rows, cols):
        return [((rows, cols), BF)] * n_dp

    def span(f):
        return slice(f * tile, (f + 1) * tile)

    def expert_body(j, n_parts, here_ref, *refs):
        parts, (w_in, w_out, gate_ref), refs = refs[:n_parts], refs[n_parts : n_parts + 3], refs[n_parts + 3 :]
        out_outs, in_outs, refs = refs[:4], refs[4:8], refs[8:]
        n_rows = len(refs) - 21
        row_outs, refs = refs[:n_rows], refs[n_rows:]
        xs, dys, act, slope, grad, w_i, w_o, *bufs = refs[:-2]
        out_bufs, in_bufs, row_bufs = bufs[:4], bufs[4:8], bufs[8:]
        reads, writes = Copies(refs[-2]), Copies(refs[-1])
        x_here = lay_out(reads, here_ref[1], parts, 0, xs)
        wi_here = [reads.start(w_in.at[j, :, span(f)], w_i.at[:, span(f)]) for f in range(tiles)]
        dy_here = lay_out(reads, here_ref[1], parts, quarter, dys)
        wo_here = reads.start(w_out.at[j], w_o)
        for copy in x_here:
            copy.wait()
        for f in range(tiles):
            at = span(f)
            wi_here[f].wait()
            pre = dot(xs[...], w_i[:, at])
            cdf = 0.5 * (1.0 + lax.erf(pre * (1.0 / math.sqrt(2.0))))
            dens = jnp.exp(-0.5 * pre * pre) * (1.0 / math.sqrt(2.0 * math.pi))
            value = (pre * cdf).astype(BF)
            slope[:, at] = (cdf + pre * dens).astype(BF)
            act[:, at] = value
            act_t = value.T
            if f == 0:
                for copy in dy_here:
                    copy.wait()
            for k in range(n_dp):
                out_bufs[k][at, :] = dot(act_t, dys[:, quarter_at(here_ref[0], k)]).astype(BF)
        for k in range(n_dp):
            writes.start(out_bufs[k], out_outs[k])
        wo_here.wait()
        total = jnp.zeros((slots, 1), F32)
        for f in range(tiles):
            at = span(f)
            back = dot_t(dys[...], w_o[at, :])
            total += jnp.sum(act[:, at].astype(F32) * back, axis=1, keepdims=True)
            grad[:, at] = (back * slope[:, at].astype(F32)).astype(BF)
        gate_ref[...] = total
        for k in (2, 1, 3, 0):
            x_t = xs[:, quarter_at(here_ref[0], k)].T
            for f in range(tiles):
                in_bufs[k][:, span(f)] = dot(x_t, grad[:, span(f)]).astype(BF)
            writes.start(in_bufs[k], in_outs[k])
        for k in (2, 1, 3, 0):
            row_bufs[k][...] = dot_t(grad[...], w_i[quarter_at(here_ref[1], k), :]).astype(BF)
            writes.start(row_bufs[k], row_outs[k] if n_rows > 1 else row_outs[0].at[(here_ref[1] + k) % n_chan])
        writes.wait_all()

    def add(a, b):
        return (a.astype(F32) + b.astype(F32)).astype(BF)

    def reduce_start(parts, axis, by):
        return [shift(parts[2], axis, by), shift(parts[-by % 4], axis, -by)]

    def reduce_end(parts, arrived, axis, by):
        return [parts[0], shift(add(parts[by % 4], arrived[0]), axis, by), arrived[1]]

    def total(terms):
        return sum(t.astype(F32) for t in terms).astype(BF)

    received = []
    for j in range(n_local):
        sent = sends[j]
        if received:
            sent, received[-1] = lax.optimization_barrier((sent, received[-1]))
        received.append(exchange(sent))
    flops = 2 * slots * width * hidden
    wide = pltpu.VMEM((slots, width), BF)
    whole = pltpu.VMEM((width, hidden), BF)
    weight_pieces = pieces(hidden, quarter) + pieces(quarter, hidden)
    row_pieces = pieces(slots, quarter)
    gates, made, arrived, out_terms, in_terms = [], [], [], [], []
    for j in range(n_local):
        parts = gather_parts(received[j], j == 0)
        if j + 1 < n_local:
            *parts, received[j + 1] = lax.optimization_barrier((*parts, received[j + 1]))
        if j:
            stacked = lax.all_to_all(made[-1][-1], "chan", split_axis=0, concat_axis=0, tiled=True)
            parts, arrived[0][0], arrived[1][0] = lax.optimization_barrier((parts, arrived[0][0], arrived[1][0]))
            back_terms = stacked
            out_terms.append(reduce_end(made[-1][:n_dp], arrived[0], "dp", 1))
            in_terms.append(reduce_end(made[-1][n_dp : 2 * n_dp], arrived[1], "dp", -1))
        results = weight_pieces + (row_pieces if j else [((n_chan, slots, quarter), BF)])
        gate_part, *results_j = call(
            functools.partial(expert_body, j, len(parts)),
            [here, *parts, in_weight, out_weight],
            [((slots, 1), F32)] + results,
            5 * flops,
            len(parts) + 2,
            len(results),
            [wide] * 5
            + [whole] * 2
            + [pltpu.VMEM(s, d) for s, d in weight_pieces + row_pieces]
            + [pltpu.SemaphoreType.DMA((2 * len(parts) + tiles + 1,)), pltpu.SemaphoreType.DMA((3 * n_dp,))],
        )
        made.append(results_j)
        gates.append(gate_part)
        arrived = [reduce_start(results_j[:n_dp], "dp", 1), reduce_start(results_j[n_dp : 2 * n_dp], "dp", -1)]
    out_terms.append(reduce_end(made[-1][:n_dp], arrived[0], "dp", 1))
    in_terms.append(reduce_end(made[-1][n_dp : 2 * n_dp], arrived[1], "dp", -1))

    row_parts = made[-1][2 * n_dp :]
    row_parts, out_terms[0], in_terms[0] = lax.optimization_barrier((row_parts, out_terms[0], in_terms[0]))
    row_arrived = reduce_start(row_parts, "chan", 1)
    gates, row_arrived[0] = lax.optimization_barrier((gates, row_arrived[0]))
    row_sums = [total([back_terms[c] for c in range(n_chan)]), total(reduce_end(row_parts, row_arrived, "chan", 1))]
    back = jnp.concatenate([r.reshape(groups, capacity, quarter) for r in row_sums], axis=1)
    rows_back = exchange(back.reshape(n_local * slots, quarter))
    out_grads = [total(t) for t in out_terms]
    in_grads = [total(t) for t in in_terms]
    gate_rows = jnp.concatenate([g.reshape(groups, capacity) for g in gates], axis=1)
    gate_rows = jnp.broadcast_to(gate_rows[:, None, :], (groups, n_chan, n_local * capacity))
    gate_rows = lax.all_to_all(
        gate_rows.reshape(groups * n_chan, n_local * capacity),
        ("expert", "chan"),
        split_axis=0,
        concat_axis=0,
        tiled=True,
    ).reshape(groups, n_chan, n_local * capacity)
    gate_rows = jnp.sum(gate_rows, axis=1).reshape(1, n_local * slots)

    def combine_body(_, routes_ref, gate_ref, sums_ref, rows_ref, token_ref, gate_out_ref):
        places = slot_places(routes_ref[...], experts, capacity)
        at = lax.broadcasted_iota(jnp.int32, (n_local * slots, toks), 0)
        hits = []
        for which, place in places:
            group = lax.div(place, capacity)
            hits.append(at == place + (group * (n_local - 1) + which) * capacity)
        pick = jnp.where(hits[0] | hits[1], 1.0, 0.0)
        token_ref[...] = dot(pick.T.astype(BF), rows_ref[...]).astype(BF)
        gate = gate_ref[...].astype(F32)
        for k in range(2):
            mask = jnp.where(hits[k], 1.0, 0.0)
            found = jnp.dot(sums_ref[...], mask, preferred_element_type=F32, precision=lax.Precision.HIGHEST)
            gate_out_ref[k : k + 1, :] = (found / gate[k : k + 1, :]).astype(BF)

    token_grads, gate_grads = call(
        combine_body,
        [here, routes.T, gate_values.T, gate_rows, rows_back],
        [((toks, quarter), BF), (gate_values.shape[::-1], BF)],
        2 * n_local * slots * toks * quarter,
    )
    gate_grads = gate_grads.T
    return (token_grads, gate_grads, jnp.stack(in_grads), jnp.stack(out_grads))


def solution(mesh):
    placed = (
        P(("dp", "expert"), "chan"),
        P(("dp", "expert"), "chan"),
        P(("dp", "expert"), None),
        P(("dp", "expert"), None),
        P("expert", None, "chan"),
        P("expert", "chan", None),
    )
    return jax.shard_map(
        on_device,
        mesh=mesh,
        in_specs=placed,
        out_specs=(
            P(("dp", "expert"), "chan"),
            P(("dp", "expert"), None),
            P("expert", "dp", "chan"),
            P("expert", "chan", "dp"),
        ),
        check_vma=False,
    )
```

```python
import functools
import math

import jax
import jax.numpy as jnp
from jax import lax
from jax.experimental import pallas as pl
from jax.experimental.pallas import tpu as pltpu
from jax.sharding import PartitionSpec as P

BF = jnp.bfloat16
F32 = jnp.float32
VMEM_BYTES = 60 * 1024 * 1024


def dot(a, b):
    return jnp.dot(a, b, preferred_element_type=F32)


def dot_t(a, b):
    return lax.dot_general(a, b, (((1,), (1,)), ((), ())), preferred_element_type=F32)


def call(body, ins, outs, flops, far_ins=0, far_outs=0, scratch=()):
    far = pl.BlockSpec(memory_space=pl.ANY)

    def specs(shapes, n_far):
        near = len(shapes) - n_far
        return [pl.BlockSpec(s, lambda i, n=len(s): (0,) * n) for s in shapes[:near]] + [far] * n_far

    moved = sum(x.size * x.dtype.itemsize for x in ins) + sum(
        math.prod(s) * jnp.dtype(d).itemsize for s, d in outs
    )
    return pl.pallas_call(
        body,
        grid=(1,),
        in_specs=[pl.BlockSpec(memory_space=pltpu.SMEM)] + specs([x.shape for x in ins[1:]], far_ins),
        out_specs=specs([s for s, _ in outs], far_outs),
        out_shape=[jax.ShapeDtypeStruct(s, d) for s, d in outs],
        scratch_shapes=scratch,
        compiler_params=pltpu.CompilerParams(vmem_limit_bytes=VMEM_BYTES),
        cost_estimate=pl.CostEstimate(flops=flops // 16, bytes_accessed=moved // 16, transcendentals=0),
    )(*ins)


class Copies:
    def __init__(self, sems):
        self.sems = sems
        self.started = []

    def start(self, source, target):
        copy = pltpu.make_async_copy(source, target, self.sems.at[len(self.started)])
        copy.start()
        self.started.append(copy)
        return copy

    def wait_all(self):
        for copy in self.started:
            copy.wait()


def slot_places(routes, experts, capacity):
    toks = routes.shape[1]
    r0 = routes[0:1, :]
    r1 = routes[1:2, :]
    expert = lax.broadcasted_iota(jnp.int32, (experts, toks), 0)
    named = jnp.where((expert == r0) | (expert == r1), 1.0, 0.0).astype(BF)
    row = lax.broadcasted_iota(jnp.int32, (toks, toks), 0)
    col = lax.broadcasted_iota(jnp.int32, (toks, toks), 1)
    earlier = jnp.where(row < col, 1.0, 0.0).astype(BF)
    before = dot(named, earlier)
    out = []
    for r in (r0, r1):
        slot = jnp.sum(jnp.where(expert == r, before, 0.0), axis=0, keepdims=True).astype(jnp.int32)
        out.append((r & 1, (r >> 1) * capacity + slot))
    return out


def matches(places, j, slots, toks):
    at = lax.broadcasted_iota(jnp.int32, (slots, toks), 0)
    return [at == jnp.where(which == j, place, -1) for which, place in places]


def on_device(tokens, out_cotangent, routes, gate_values, in_weight, out_weight):
    toks, quarter = tokens.shape
    groups = lax.axis_size("expert")
    n_local = in_weight.shape[0]
    experts = n_local * groups
    capacity = min(toks, 4 * toks // experts)
    slots = groups * capacity
    width, hidden = in_weight.shape[1:]
    n_chan = lax.axis_size("chan")
    half = slots // 2
    here = jnp.stack([lax.axis_index("dp"), lax.axis_index("chan")]).astype(jnp.int32)

    def shift(x, axis, by):
        n = lax.axis_size(axis)
        return lax.ppermute(x, axis, [(i, (i + by) % n) for i in range(n)])

    def pack_body(_, x_ref, dy_ref, routes_ref, gate_ref, *send_refs):
        places = slot_places(routes_ref[...], experts, capacity)
        gate = gate_ref[...].astype(F32)
        x = x_ref[...]
        dy = dy_ref[...]
        for j in range(n_local):
            m0, m1 = matches(places, j, slots, toks)
            pick = jnp.where(m0 | m1, 1.0, 0.0)
            gated = jnp.where(m0, gate[0:1, :], 0.0) + jnp.where(m1, gate[1:2, :], 0.0)
            send_refs[j][:, :quarter] = dot(pick.astype(BF), x).astype(BF)
            send_refs[j][:, quarter:] = dot(gated.astype(BF), dy).astype(BF)

    sends = call(
        pack_body,
        [here, tokens, out_cotangent, routes.T, gate_values.T],
        [((slots, 2 * quarter), BF)] * n_local,
        4 * n_local * slots * toks * quarter,
    )

    def exchange(x):
        return lax.all_to_all(
            x.reshape(groups, x.shape[0] // groups, x.shape[1]), "expert", split_axis=0, concat_axis=0, tiled=True
        ).reshape(x.shape)

    def gather_parts(x, in_halves):
        xa, xb = x[:half], x[half:]
        if in_halves:
            left_a = shift(xa, "chan", 1)
            right_b = shift(xb, "chan", -1)
            near = [xa, xb, left_a, shift(xb, "chan", 1), shift(xa, "chan", -1), right_b]
        else:
            left = shift(x, "chan", 1)
            right = shift(x, "chan", -1)
            left_a, right_b = left[:half], right[half:]
            near = [x, left, right]
        return [*near, shift(left_a, "chan", 1), shift(right_b, "chan", -1)]

    def lay_out(copies, c, refs, first, full_ref):
        took = slice(first, first + quarter)
        started = []
        at = 0
        for k in (0, n_chan - 1, 1, 2):
            cols = pl.ds(pl.multiple_of(((c + k) % n_chan) * quarter, quarter), quarter)
            row = 0
            while row < slots:
                rows = refs[at].shape[0]
                started.append(copies.start(refs[at].at[:, took], full_ref.at[row : row + rows, cols]))
                row += rows
                at += 1
        return started

    tile = 512
    tiles = hidden // tile
    n_dp = lax.axis_size("dp")

    def quarter_at(c, k):
        return pl.ds(pl.multiple_of(((c + k) % n_dp) * quarter, quarter), quarter)

    def pieces(rows, cols):
        return [((rows, cols), BF)] * n_dp

    def span(f):
        return slice(f * tile, (f + 1) * tile)

    def expert_body(j, n_parts, here_ref, *refs):
        parts, (w_in, w_out, gate_ref), refs = refs[:n_parts], refs[n_parts : n_parts + 3], refs[n_parts + 3 :]
        out_outs, in_outs, refs = refs[:4], refs[4:8], refs[8:]
        n_rows = len(refs) - 21
        row_outs, refs = refs[:n_rows], refs[n_rows:]
        xs, dys, act, slope, grad, w_i, w_o, *bufs = refs[:-2]
        out_bufs, in_bufs, row_bufs = bufs[:4], bufs[4:8], bufs[8:]
        reads, writes = Copies(refs[-2]), Copies(refs[-1])
        x_here = lay_out(reads, here_ref[1], parts, 0, xs)
        wi_here = [reads.start(w_in.at[j, :, span(f)], w_i.at[:, span(f)]) for f in range(tiles)]
        dy_here = lay_out(reads, here_ref[1], parts, quarter, dys)
        wo_here = reads.start(w_out.at[j], w_o)
        for copy in x_here:
            copy.wait()
        for f in range(tiles):
            at = span(f)
            wi_here[f].wait()
            pre = dot(xs[...], w_i[:, at])
            cdf = 0.5 * (1.0 + lax.erf(pre * (1.0 / math.sqrt(2.0))))
            dens = jnp.exp(-0.5 * pre * pre) * (1.0 / math.sqrt(2.0 * math.pi))
            value = (pre * cdf).astype(BF)
            slope[:, at] = (cdf + pre * dens).astype(BF)
            act[:, at] = value
            act_t = value.T
            if f == 0:
                for copy in dy_here:
                    copy.wait()
            for k in range(n_dp):
                out_bufs[k][at, :] = dot(act_t, dys[:, quarter_at(here_ref[0], k)]).astype(BF)
        for k in range(n_dp):
            writes.start(out_bufs[k], out_outs[k])
        wo_here.wait()
        total = jnp.zeros((slots, 1), F32)
        for f in range(tiles):
            at = span(f)
            back = dot_t(dys[...], w_o[at, :])
            total += jnp.sum(act[:, at].astype(F32) * back, axis=1, keepdims=True)
            grad[:, at] = (back * slope[:, at].astype(F32)).astype(BF)
        gate_ref[...] = total
        for k in (2, 1, 3, 0):
            x_t = xs[:, quarter_at(here_ref[0], k)].T
            for f in range(tiles):
                in_bufs[k][:, span(f)] = dot(x_t, grad[:, span(f)]).astype(BF)
            writes.start(in_bufs[k], in_outs[k])
        for k in (2, 1, 3, 0):
            row_bufs[k][...] = dot_t(grad[...], w_i[quarter_at(here_ref[1], k), :]).astype(BF)
            writes.start(row_bufs[k], row_outs[k] if n_rows > 1 else row_outs[0].at[(here_ref[1] + k) % n_chan])
        writes.wait_all()

    def add(a, b):
        return (a.astype(F32) + b.astype(F32)).astype(BF)

    def reduce_start(parts, axis, by):
        return [shift(parts[2], axis, by), shift(parts[-by % 4], axis, -by)]

    def reduce_end(parts, arrived, axis, by):
        return [parts[0], shift(add(parts[by % 4], arrived[0]), axis, by), arrived[1]]

    def total(terms):
        return sum(t.astype(F32) for t in terms).astype(BF)

    received = []
    for j in range(n_local):
        sent = sends[j]
        if received:
            sent, received[-1] = lax.optimization_barrier((sent, received[-1]))
        received.append(exchange(sent))
    flops = 2 * slots * width * hidden
    wide = pltpu.VMEM((slots, width), BF)
    whole = pltpu.VMEM((width, hidden), BF)
    weight_pieces = pieces(hidden, quarter) + pieces(quarter, hidden)
    row_pieces = pieces(slots, quarter)
    gates, made, arrived, out_terms, in_terms = [], [], [], [], []
    for j in range(n_local):
        parts = gather_parts(received[j], j == 0)
        if j + 1 < n_local:
            *parts, received[j + 1] = lax.optimization_barrier((*parts, received[j + 1]))
        if j:
            stacked = lax.all_to_all(made[-1][-1], "chan", split_axis=0, concat_axis=0, tiled=True)
            parts, arrived[0][0], arrived[1][0] = lax.optimization_barrier((parts, arrived[0][0], arrived[1][0]))
            back_terms = stacked
            out_terms.append(reduce_end(made[-1][:n_dp], arrived[0], "dp", 1))
            in_terms.append(reduce_end(made[-1][n_dp : 2 * n_dp], arrived[1], "dp", -1))
        results = weight_pieces + (row_pieces if j else [((n_chan, slots, quarter), BF)])
        gate_part, *results_j = call(
            functools.partial(expert_body, j, len(parts)),
            [here, *parts, in_weight, out_weight],
            [((slots, 1), F32)] + results,
            5 * flops,
            len(parts) + 2,
            len(results),
            [wide] * 5
            + [whole] * 2
            + [pltpu.VMEM(s, d) for s, d in weight_pieces + row_pieces]
            + [pltpu.SemaphoreType.DMA((2 * len(parts) + tiles + 1,)), pltpu.SemaphoreType.DMA((3 * n_dp,))],
        )
        made.append(results_j)
        gates.append(gate_part)
        if j:
            fars = [results_j[3], results_j[n_dp + 1], results_j[2 * n_dp + 3]]
            fars, out_terms[0], in_terms[0] = lax.optimization_barrier((fars, out_terms[0], in_terms[0]))
            results_j[3], results_j[n_dp + 1], results_j[2 * n_dp + 3] = fars
        arrived = [reduce_start(results_j[:n_dp], "dp", 1), reduce_start(results_j[n_dp : 2 * n_dp], "dp", -1)]
    gates, arrived[1][0] = lax.optimization_barrier((gates, arrived[1][0]))
    out_terms.append(reduce_end(made[-1][:n_dp], arrived[0], "dp", 1))
    in_terms.append(reduce_end(made[-1][n_dp : 2 * n_dp], arrived[1], "dp", -1))

    row_parts = made[-1][2 * n_dp :]
    row_parts[2], in_terms[0], out_terms[0] = lax.optimization_barrier((row_parts[2], in_terms[0], out_terms[0]))
    row_arrived = reduce_start(row_parts, "chan", 1)
    row_sums = [total([back_terms[c] for c in range(n_chan)]), total(reduce_end(row_parts, row_arrived, "chan", 1))]
    back = jnp.concatenate([r.reshape(groups, capacity, quarter) for r in row_sums], axis=1)
    rows_back = exchange(back.reshape(n_local * slots, quarter))
    out_grads = [total(t) for t in out_terms]
    in_grads = [total(t) for t in in_terms]
    gate_rows = jnp.concatenate([g.reshape(groups, capacity) for g in gates], axis=1)
    gate_rows = jnp.broadcast_to(gate_rows[:, None, :], (groups, n_chan, n_local * capacity))
    gate_rows = lax.all_to_all(
        gate_rows.reshape(groups * n_chan, n_local * capacity),
        ("expert", "chan"),
        split_axis=0,
        concat_axis=0,
        tiled=True,
    ).reshape(groups, n_chan, n_local * capacity)
    gate_rows = jnp.sum(gate_rows, axis=1).reshape(1, n_local * slots)

    def combine_body(_, routes_ref, gate_ref, sums_ref, rows_ref, token_ref, gate_out_ref):
        places = slot_places(routes_ref[...], experts, capacity)
        at = lax.broadcasted_iota(jnp.int32, (n_local * slots, toks), 0)
        hits = []
        for which, place in places:
            group = lax.div(place, capacity)
            hits.append(at == place + (group * (n_local - 1) + which) * capacity)
        pick = jnp.where(hits[0] | hits[1], 1.0, 0.0)
        token_ref[...] = dot(pick.T.astype(BF), rows_ref[...]).astype(BF)
        gate = gate_ref[...].astype(F32)
        for k in range(2):
            mask = jnp.where(hits[k], 1.0, 0.0)
            found = jnp.dot(sums_ref[...], mask, preferred_element_type=F32, precision=lax.Precision.HIGHEST)
            gate_out_ref[k : k + 1, :] = (found / gate[k : k + 1, :]).astype(BF)

    token_grads, gate_grads = call(
        combine_body,
        [here, routes.T, gate_values.T, gate_rows, rows_back],
        [((toks, quarter), BF), (gate_values.shape[::-1], BF)],
        2 * n_local * slots * toks * quarter,
    )
    gate_grads = gate_grads.T
    return (token_grads, gate_grads, jnp.stack(in_grads), jnp.stack(out_grads))


def solution(mesh):
    placed = (
        P(("dp", "expert"), "chan"),
        P(("dp", "expert"), "chan"),
        P(("dp", "expert"), None),
        P(("dp", "expert"), None),
        P("expert", None, "chan"),
        P("expert", "chan", None),
    )
    return jax.shard_map(
        on_device,
        mesh=mesh,
        in_specs=placed,
        out_specs=(
            P(("dp", "expert"), "chan"),
            P(("dp", "expert"), None),
            P("expert", "dp", "chan"),
            P("expert", "chan", "dp"),
        ),
        check_vma=False,
    )
```

```python
import functools
import math

import jax
import jax.numpy as jnp
from jax import lax
from jax.experimental import pallas as pl
from jax.experimental.pallas import tpu as pltpu
from jax.sharding import PartitionSpec as P

BF = jnp.bfloat16
F32 = jnp.float32
VMEM_BYTES = 60 * 1024 * 1024


def dot(a, b):
    return jnp.dot(a, b, preferred_element_type=F32)


def dot_t(a, b):
    return lax.dot_general(a, b, (((1,), (1,)), ((), ())), preferred_element_type=F32)


def call(body, ins, outs, flops, far_ins=0, far_outs=0, scratch=()):
    far = pl.BlockSpec(memory_space=pl.ANY)

    def specs(shapes, n_far):
        near = len(shapes) - n_far
        return [pl.BlockSpec(s, lambda i, n=len(s): (0,) * n) for s in shapes[:near]] + [far] * n_far

    moved = sum(x.size * x.dtype.itemsize for x in ins) + sum(
        math.prod(s) * jnp.dtype(d).itemsize for s, d in outs
    )
    return pl.pallas_call(
        body,
        grid=(1,),
        in_specs=[pl.BlockSpec(memory_space=pltpu.SMEM)] + specs([x.shape for x in ins[1:]], far_ins),
        out_specs=specs([s for s, _ in outs], far_outs),
        out_shape=[jax.ShapeDtypeStruct(s, d) for s, d in outs],
        scratch_shapes=scratch,
        compiler_params=pltpu.CompilerParams(vmem_limit_bytes=VMEM_BYTES),
        cost_estimate=pl.CostEstimate(flops=flops // 16, bytes_accessed=moved // 16, transcendentals=0),
    )(*ins)


class Copies:
    def __init__(self, sems):
        self.sems = sems
        self.started = []

    def start(self, source, target):
        copy = pltpu.make_async_copy(source, target, self.sems.at[len(self.started)])
        copy.start()
        self.started.append(copy)
        return copy

    def wait_all(self):
        for copy in self.started:
            copy.wait()


def slot_places(routes, experts, capacity):
    toks = routes.shape[1]
    r0 = routes[0:1, :]
    r1 = routes[1:2, :]
    expert = lax.broadcasted_iota(jnp.int32, (experts, toks), 0)
    named = jnp.where((expert == r0) | (expert == r1), 1.0, 0.0).astype(BF)
    row = lax.broadcasted_iota(jnp.int32, (toks, toks), 0)
    col = lax.broadcasted_iota(jnp.int32, (toks, toks), 1)
    earlier = jnp.where(row < col, 1.0, 0.0).astype(BF)
    before = dot(named, earlier)
    out = []
    for r in (r0, r1):
        slot = jnp.sum(jnp.where(expert == r, before, 0.0), axis=0, keepdims=True).astype(jnp.int32)
        out.append((r & 1, (r >> 1) * capacity + slot))
    return out


def matches(places, j, slots, toks):
    at = lax.broadcasted_iota(jnp.int32, (slots, toks), 0)
    return [at == jnp.where(which == j, place, -1) for which, place in places]


def on_device(tokens, out_cotangent, routes, gate_values, in_weight, out_weight):
    toks, quarter = tokens.shape
    groups = lax.axis_size("expert")
    n_local = in_weight.shape[0]
    experts = n_local * groups
    capacity = min(toks, 4 * toks // experts)
    slots = groups * capacity
    width, hidden = in_weight.shape[1:]
    n_chan = lax.axis_size("chan")
    half = slots // 2
    here = jnp.stack([lax.axis_index("dp"), lax.axis_index("chan")]).astype(jnp.int32)

    def shift(x, axis, by):
        n = lax.axis_size(axis)
        return lax.ppermute(x, axis, [(i, (i + by) % n) for i in range(n)])

    def pack_body(_, x_ref, dy_ref, routes_ref, gate_ref, *send_refs):
        places = slot_places(routes_ref[...], experts, capacity)
        gate = gate_ref[...].astype(F32)
        x = x_ref[...]
        dy = dy_ref[...]
        for j in range(n_local):
            m0, m1 = matches(places, j, slots, toks)
            pick = jnp.where(m0 | m1, 1.0, 0.0)
            gated = jnp.where(m0, gate[0:1, :], 0.0) + jnp.where(m1, gate[1:2, :], 0.0)
            send_refs[j][:, :quarter] = dot(pick.astype(BF), x).astype(BF)
            send_refs[j][:, quarter:] = dot(gated.astype(BF), dy).astype(BF)

    sends = call(
        pack_body,
        [here, tokens, out_cotangent, routes.T, gate_values.T],
        [((slots, 2 * quarter), BF)] * n_local,
        4 * n_local * slots * toks * quarter,
    )

    def exchange(x):
        return lax.all_to_all(
            x.reshape(groups, x.shape[0] // groups, x.shape[1]), "expert", split_axis=0, concat_axis=0, tiled=True
        ).reshape(x.shape)

    def gather_parts(x, in_halves):
        xa, xb = x[:half], x[half:]
        if in_halves:
            left_a = shift(xa, "chan", 1)
            right_b = shift(xb, "chan", -1)
            near = [xa, xb, left_a, shift(xb, "chan", 1), shift(xa, "chan", -1), right_b]
        else:
            left = shift(x, "chan", 1)
            right = shift(x, "chan", -1)
            left_a, right_b = left[:half], right[half:]
            near = [x, left, right]
        return [*near, shift(left_a, "chan", 1), shift(right_b, "chan", -1)]

    def lay_out(copies, c, refs, first, full_ref):
        took = slice(first, first + quarter)
        started = []
        at = 0
        for k in (0, n_chan - 1, 1, 2):
            cols = pl.ds(pl.multiple_of(((c + k) % n_chan) * quarter, quarter), quarter)
            row = 0
            while row < slots:
                rows = refs[at].shape[0]
                started.append(copies.start(refs[at].at[:, took], full_ref.at[row : row + rows, cols]))
                row += rows
                at += 1
        return started

    tile = 512
    tiles = hidden // tile
    n_dp = lax.axis_size("dp")

    def quarter_at(c, k):
        return pl.ds(pl.multiple_of(((c + k) % n_dp) * quarter, quarter), quarter)

    def pieces(rows, cols):
        return [((rows, cols), BF)] * n_dp

    def span(f):
        return slice(f * tile, (f + 1) * tile)

    def expert_body(j, n_parts, here_ref, *refs):
        parts, (w_in, w_out, gate_ref), refs = refs[:n_parts], refs[n_parts : n_parts + 3], refs[n_parts + 3 :]
        out_outs, in_outs, refs = refs[:4], refs[4:8], refs[8:]
        n_rows = len(refs) - 21
        row_outs, refs = refs[:n_rows], refs[n_rows:]
        xs, dys, act, slope, grad, w_i, w_o, *bufs = refs[:-2]
        out_bufs, in_bufs, row_bufs = bufs[:4], bufs[4:8], bufs[8:]
        reads, writes = Copies(refs[-2]), Copies(refs[-1])
        x_here = lay_out(reads, here_ref[1], parts, 0, xs)
        wi_here = [reads.start(w_in.at[j, :, span(f)], w_i.at[:, span(f)]) for f in range(tiles)]
        dy_here = lay_out(reads, here_ref[1], parts, quarter, dys)
        wo_here = reads.start(w_out.at[j], w_o)
        for copy in x_here:
            copy.wait()
        for f in range(tiles):
            at = span(f)
            wi_here[f].wait()
            pre = dot(xs[...], w_i[:, at])
            cdf = 0.5 * (1.0 + lax.erf(pre * (1.0 / math.sqrt(2.0))))
            dens = jnp.exp(-0.5 * pre * pre) * (1.0 / math.sqrt(2.0 * math.pi))
            value = (pre * cdf).astype(BF)
            slope[:, at] = (cdf + pre * dens).astype(BF)
            act[:, at] = value
            act_t = value.T
            if f == 0:
                for copy in dy_here:
                    copy.wait()
            for k in range(n_dp):
                out_bufs[k][at, :] = dot(act_t, dys[:, quarter_at(here_ref[0], k)]).astype(BF)
        for k in range(n_dp):
            writes.start(out_bufs[k], out_outs[k])
        wo_here.wait()
        total = jnp.zeros((slots, 1), F32)
        for f in range(tiles):
            at = span(f)
            back = dot_t(dys[...], w_o[at, :])
            total += jnp.sum(act[:, at].astype(F32) * back, axis=1, keepdims=True)
            grad[:, at] = (back * slope[:, at].astype(F32)).astype(BF)
        gate_ref[...] = total
        for k in (2, 1, 3, 0):
            x_t = xs[:, quarter_at(here_ref[0], k)].T
            for f in range(tiles):
                in_bufs[k][:, span(f)] = dot(x_t, grad[:, span(f)]).astype(BF)
            writes.start(in_bufs[k], in_outs[k])
        for k in (2, 1, 3, 0):
            row_bufs[k][...] = dot_t(grad[...], w_i[quarter_at(here_ref[1], k), :]).astype(BF)
            writes.start(row_bufs[k], row_outs[k] if n_rows > 1 else row_outs[0].at[(here_ref[1] + k) % n_chan])
        writes.wait_all()

    def add(a, b):
        return (a.astype(F32) + b.astype(F32)).astype(BF)

    def reduce_start(parts, axis, by):
        return [shift(parts[2], axis, by), shift(parts[-by % 4], axis, -by)]

    def reduce_end(parts, arrived, axis, by):
        return [parts[0], shift(add(parts[by % 4], arrived[0]), axis, by), arrived[1]]

    def total(terms):
        return sum(t.astype(F32) for t in terms).astype(BF)

    received = []
    for j in range(n_local):
        sent = sends[j]
        if received:
            sent, received[-1] = lax.optimization_barrier((sent, received[-1]))
        received.append(exchange(sent))
    flops = 2 * slots * width * hidden
    wide = pltpu.VMEM((slots, width), BF)
    whole = pltpu.VMEM((width, hidden), BF)
    weight_pieces = pieces(hidden, quarter) + pieces(quarter, hidden)
    row_pieces = pieces(slots, quarter)
    gates, made, arrived, out_terms, in_terms = [], [], [], [], []
    for j in range(n_local):
        parts = gather_parts(received[j], j == 0)
        if j + 1 < n_local:
            *parts, received[j + 1] = lax.optimization_barrier((*parts, received[j + 1]))
        if j:
            stacked = lax.all_to_all(made[-1][-1], "chan", split_axis=0, concat_axis=0, tiled=True)
            parts, arrived[0][0], arrived[1][0] = lax.optimization_barrier((parts, arrived[0][0], arrived[1][0]))
            back_terms = stacked
            out_terms.append(reduce_end(made[-1][:n_dp], arrived[0], "dp", 1))
            in_terms.append(reduce_end(made[-1][n_dp : 2 * n_dp], arrived[1], "dp", -1))
        results = weight_pieces + (row_pieces if j else [((n_chan, slots, quarter), BF)])
        gate_part, *results_j = call(
            functools.partial(expert_body, j, len(parts)),
            [here, *parts, in_weight, out_weight],
            [((slots, 1), F32)] + results,
            5 * flops,
            len(parts) + 2,
            len(results),
            [wide] * 5
            + [whole] * 2
            + [pltpu.VMEM(s, d) for s, d in weight_pieces + row_pieces]
            + [pltpu.SemaphoreType.DMA((2 * len(parts) + tiles + 1,)), pltpu.SemaphoreType.DMA((3 * n_dp,))],
        )
        made.append(results_j)
        gates.append(gate_part)
        if j:
            fars = [results_j[3], results_j[n_dp + 1]]
            fars, out_terms[0], in_terms[0] = lax.optimization_barrier((fars, out_terms[0], in_terms[0]))
            results_j[3], results_j[n_dp + 1] = fars
        arrived = [reduce_start(results_j[:n_dp], "dp", 1), reduce_start(results_j[n_dp : 2 * n_dp], "dp", -1)]
    gates, arrived[1][0] = lax.optimization_barrier((gates, arrived[1][0]))
    out_terms.append(reduce_end(made[-1][:n_dp], arrived[0], "dp", 1))
    in_terms.append(reduce_end(made[-1][n_dp : 2 * n_dp], arrived[1], "dp", -1))

    row_parts = made[-1][2 * n_dp :]
    row_parts[2], in_terms[0], out_terms[0] = lax.optimization_barrier((row_parts[2], in_terms[0], out_terms[0]))
    opposite, row_parts[3] = lax.optimization_barrier((shift(row_parts[2], "chan", 1), row_parts[3]))
    row_arrived = [opposite, shift(row_parts[3], "chan", -1)]
    row_sums = [total([back_terms[c] for c in range(n_chan)]), total(reduce_end(row_parts, row_arrived, "chan", 1))]
    back = jnp.concatenate([r.reshape(groups, capacity, quarter) for r in row_sums], axis=1)
    rows_back = exchange(back.reshape(n_local * slots, quarter))
    out_grads = [total(t) for t in out_terms]
    in_grads = [total(t) for t in in_terms]
    gate_rows = jnp.concatenate([g.reshape(groups, capacity) for g in gates], axis=1)
    gate_rows = jnp.broadcast_to(gate_rows[:, None, :], (groups, n_chan, n_local * capacity))
    gate_rows = lax.all_to_all(
        gate_rows.reshape(groups * n_chan, n_local * capacity),
        ("expert", "chan"),
        split_axis=0,
        concat_axis=0,
        tiled=True,
    ).reshape(groups, n_chan, n_local * capacity)
    gate_rows = jnp.sum(gate_rows, axis=1).reshape(1, n_local * slots)

    def find(routes_ref):
        at = lax.broadcasted_iota(jnp.int32, (n_local * slots, toks), 0)
        hits = []
        for which, place in slot_places(routes_ref[...], experts, capacity):
            group = lax.div(place, capacity)
            hits.append(at == place + (group * (n_local - 1) + which) * capacity)
        return hits

    def gate_body(_, routes_ref, gate_ref, sums_ref, gate_out_ref, pick_ref):
        hits = find(routes_ref)
        pick_ref[...] = jnp.where(hits[0] | hits[1], 1.0, 0.0).T.astype(BF)
        gate = gate_ref[...].astype(F32)
        for k in range(2):
            mask = jnp.where(hits[k], 1.0, 0.0)
            found = jnp.dot(sums_ref[...], mask, preferred_element_type=F32, precision=lax.Precision.HIGHEST)
            gate_out_ref[k : k + 1, :] = (found / gate[k : k + 1, :]).astype(BF)

    gate_grads, pick = call(
        gate_body,
        [here, routes.T, gate_values.T, gate_rows],
        [(gate_values.shape[::-1], BF), ((toks, n_local * slots), BF)],
        n_local * slots * toks,
    )

    def combine_body(_, pick_ref, rows_ref, token_ref):
        token_ref[...] = dot(pick_ref[...], rows_ref[...]).astype(BF)

    (token_grads,) = call(
        combine_body,
        [here, pick, rows_back],
        [((toks, quarter), BF)],
        2 * n_local * slots * toks * quarter,
    )
    gate_grads = gate_grads.T
    return (token_grads, gate_grads, jnp.stack(in_grads), jnp.stack(out_grads))


def solution(mesh):
    placed = (
        P(("dp", "expert"), "chan"),
        P(("dp", "expert"), "chan"),
        P(("dp", "expert"), None),
        P(("dp", "expert"), None),
        P("expert", None, "chan"),
        P("expert", "chan", None),
    )
    return jax.shard_map(
        on_device,
        mesh=mesh,
        in_specs=placed,
        out_specs=(
            P(("dp", "expert"), "chan"),
            P(("dp", "expert"), None),
            P("expert", "dp", "chan"),
            P("expert", "chan", "dp"),
        ),
        check_vma=False,
    )
```
